32 devices in a mesh: dom: 8 (over y, x, core), blk: 4 (over z).
Axes of the slice: x: 2, y: 2, z: 4, core: 2. Of those that a mesh axis runs over, the one named last changes fastest.
Arguments:
- positions: float32 [3, 65536], P(None, ('dom', 'blk')), may hold values from -0.5 to 0.5
- strength: float32 [3, 65536], P(None, ('dom', 'blk')), may hold values from -0.18 to 0.18
- core_radius: float32 [65536], P(('dom', 'blk')), may hold values from 0.15 to 0.3
- dye_amount: float32 [65536], P(('dom', 'blk')), may hold values from -0.18 to 0.18
- cell_fraction: float32 [3, 65536], P(None, ('dom', 'blk')), may hold values from 0 to 1
- cell_index: int32 [65536], P(('dom', 'blk')), may hold values from 0 to 127
- tile_local: int32 [65536], P(('dom', 'blk')), may hold values from 0 to 15
- owner_dom: int32 [65536, 1], P(('dom', 'blk')), may hold values from 0 to 7; in each aligned block of 2048 rows (0 to 2047, 2048 to 4095, ...) at most 1280 rows name the same one
Outputs:
- velocity: float32 [3, 65536], P(None, ('dom', 'blk'))
- tile_grid: float32 [512, 4, 128], P(('dom', 'blk'))
The draws below stay inside these ranges and needn't reach their ends.
Inputs may be any that keep to these rules, and one draw needn't show every extreme that they name: `owner_dom`: in every block of 2048 rows of one device no value appears more than 1280 times, and in some block a value appears exactly 1280 times.
All inputs are finite; a program needn't handle non-finite values.
Results may differ from the reference program's by a relative error of at most 0.0003.
Values sent between devices are 32-bit elements; how exact they have to be, the bound alone decides.
No kernel may reach another device: no remote copies, remote signals or barrier semaphores. Data moves between devices by JAX's collectives and lax.ppermute only.
A program may use at most 64 MiB of HBM per device.

```python
import math
import jax
import jax.numpy as jnp
import numpy as np
from jax import lax

PD = 2048
P_SIZE = 65536
REGION = 8192
TPD = 16
TILES = 512
CAP = 1280
N_DOM = 8
N_BLK = 4


def with_ends(array, stream_key, low, high):
    shape = array.shape
    place = [jax.random.randint(jax.random.fold_in(stream_key, axis), (), 0, shape[axis]) for axis in range(len(shape))]
    array = array.at[tuple(place)].set(low)
    longest = shape.index(max(shape))
    place[longest] = (place[longest] + 1) % shape[longest]
    return array.at[tuple(place)].set(high)


def level_of(rng, dims, cuts, least, largest):
    factor_of, own = 1.0, jax.random.fold_in(rng, 6)
    for dim, blocks in cuts:
        heights = jnp.exp(jax.random.uniform(jax.random.fold_in(own, dim), (blocks,), jnp.float32, least / len(cuts), largest / len(cuts)))
        factor_of = factor_of * jnp.repeat(heights, dims[dim] // blocks).reshape([-1 if axis == dim else 1 for axis in range(len(dims))])
    return factor_of


def routed_block(stream_key, own, number, rows, number_of, top, limit, skew):
    order = jax.random.permutation(stream_key, number_of)
    packed, common = shares(number_of, rows * top, limit, skew, True), shares(number_of, rows * top, limit, skew, False)
    places = jnp.arange(number_of)

    def named(tallies, offset_by):
        used = int((tallies > 0).sum())
        fixed = max(1, used // 4)
        moved = fixed + (places - fixed + offset_by * (used - fixed)) % max(1, number_of - fixed)
        return jnp.zeros((number_of,), jnp.int32).at[order[jnp.where(places < fixed, places, moved)]].set(jnp.asarray(tallies, jnp.int32))

    tallies = jnp.where(number % 4 == 0, named(packed, number // 4), named(common, number - number // 4 - 1))
    mixed = jax.random.permutation(jax.random.fold_in(own, 3), number_of)
    donor, sink = mixed[0:number_of // 2 * 2:2], mixed[1:number_of // 2 * 2:2]
    room = jnp.minimum(tallies[donor] - 1, limit - tallies[sink]) // 2
    room = jnp.where((donor == order[0]) | (sink == order[0]) | (tallies[sink] == 0), 0, jnp.maximum(room, 0))
    moved = jax.random.randint(jax.random.fold_in(own, 4), (number_of // 2,), 0, 1 << 20) % (room + 1)
    tallies = tallies.at[donor].add(-moved).at[sink].add(moved)
    items = jnp.searchsorted(jnp.cumsum(tallies), jnp.arange(rows * top), side="right").astype(jnp.int32)
    table = items.reshape(top, rows).T
    table = table[jax.random.permutation(jax.random.fold_in(own, 1), rows)]
    offset_by = jax.random.randint(jax.random.fold_in(own, 2), (rows, 1), 0, top)
    return jnp.take_along_axis(table, (jnp.arange(top)[None, :] + offset_by) % top, axis=1)


def shares(number_of, total, reach, slope, full):
    weights = [(1 << 20) // math.isqrt(rank ** slope) + 1 for rank in range(1, number_of + 1)]
    largest = reach if full else min(reach, max(-(-total // number_of), total * weights[0] // sum(weights)))
    least = 1 if total - largest >= number_of - 1 else 0
    counts, spare = [largest] + [least] * (number_of - 1), total - largest - least * (number_of - 1)
    while spare > 0:
        free = [i for i in range(1, number_of) if counts[i] < largest] or [i for i in range(1, number_of) if counts[i] < reach]
        pool, budget = sum([weights[i] for i in free]), spare
        for i in free:
            extra = min(reach - counts[i], max(1, budget * weights[i] // pool), spare)
            counts[i] = counts[i] + extra
            spare = spare - extra
    return np.array(counts)


def centred(key, extent, deviation, bound, cuts=(), kind=jnp.bfloat16):
    array = jax.random.normal(key, extent, jnp.float32) * deviation
    if len(cuts) > 0:
        array = level_of(key, extent, cuts, -0.22, 0.18) * array
    return jnp.clip(array, min=-bound, max=bound).astype(kind)


def setup_inputs(seed: int = 0) -> dict:
    keys = jax.random.split(jax.random.key(seed), 9)
    positions = jnp.clip(jax.random.uniform(keys[0], (3, P_SIZE), jnp.float32, -0.5, 0.5) * level_of(keys[0], (3, P_SIZE), ((1, 32),), -0.4, 0.0), -0.5, 0.5)
    strength = centred(keys[1], (3, P_SIZE), 0.03, 0.18, ((1, 32),), jnp.float32)
    core_radius = jnp.clip(jnp.exp(math.log(0.3) - 0.6931472 * jax.random.uniform(keys[2], (P_SIZE,), jnp.float32) ** level_of(keys[2], (P_SIZE,), ((0, 32),), -0.2, 0.2)), 0.15, 0.3)
    dye_amount = centred(keys[3], (P_SIZE,), 0.03, 0.18, ((0, 32),), jnp.float32)
    cell_fraction = jnp.clip(1.0 * jax.random.uniform(keys[4], (3, P_SIZE), jnp.float32) ** level_of(keys[4], (3, P_SIZE), ((1, 32),), -0.2, 0.2), 0.0, 1.0)
    cell_index = with_ends(jax.random.randint(keys[5], (P_SIZE,), 0, 128), jax.random.fold_in(keys[5], 1), 0, 127).astype(jnp.int32)
    tile_local = with_ends(jax.random.randint(keys[6], (P_SIZE,), 0, TPD), jax.random.fold_in(keys[6], 1), 0, TPD - 1).astype(jnp.int32)
    owner_dom_keys = jax.random.split(jax.random.fold_in(keys[7], 1), P_SIZE // PD)
    owner_dom_turns = jax.random.permutation(jax.random.fold_in(keys[7], 3), P_SIZE // PD)
    owner_dom = jax.vmap(lambda own, number: routed_block(jax.random.fold_in(keys[7], 2), own, number, PD, N_DOM, 1, CAP, 3))(owner_dom_keys, owner_dom_turns).reshape((P_SIZE, 1))
    return dict(positions=positions, strength=strength, core_radius=core_radius, dye_amount=dye_amount, cell_fraction=cell_fraction, cell_index=cell_index, tile_local=tile_local, owner_dom=owner_dom)


time_step = 0.02
move_scale = 2.0
inverse_volume = 32.0
kernel_scale = 1.0 / (4.0 * math.pi)
highest = lax.Precision.HIGHEST

def cross_product(left_vec, right_vec):
    return jnp.stack([left_vec[1] * right_vec[2] - left_vec[2] * right_vec[1], left_vec[2] * right_vec[0] - left_vec[0] * right_vec[2], left_vec[0] * right_vec[1] - left_vec[1] * right_vec[0]])

def pair_sums(partial_value, source_block, target_rows):
    points = source_block[0:3]
    vortex = source_block[3:6]
    radius = source_block[6]
    source_rows = jnp.concatenate([-2.0 * points, (lax.optimization_barrier(jnp.sum(points * points, axis=0)) + radius * radius)[None], jnp.ones_like(radius)[None]], axis=0)
    square = lax.dot_general(source_rows, target_rows, (((0,), (0,)), ((), ())), precision=highest, preferred_element_type=jnp.float32)
    inverse = lax.rsqrt(square)
    kernel_vals = kernel_scale * inverse * inverse * inverse
    slope_vals = -3.0 * kernel_vals * inverse * inverse
    crossed = cross_product(vortex, points)
    moment_one = (points[:, None, :] * vortex[None, :, :]).reshape(9, -1)
    moment_two = (points[:, None, :] * crossed[None, :, :]).reshape(9, -1)
    first_rows = jnp.concatenate([vortex, crossed], axis=0)
    second_rows = jnp.concatenate([vortex, crossed, moment_one, moment_two], axis=0)
    first = partial_value[0] + jnp.dot(first_rows, kernel_vals, precision=highest, preferred_element_type=jnp.float32)
    second = partial_value[1] + jnp.dot(second_rows, slope_vals, precision=highest, preferred_element_type=jnp.float32)
    return (first, second)

def block_fold(running, sources, target_rows):
    overall = sources.shape[1]
    block_width = math.gcd(overall, 1024)
    blocks = sources.reshape(7, overall // block_width, block_width).transpose(1, 0, 2)

    def scan_step(partial_value, source_block):
        return (pair_sums(partial_value, source_block, target_rows), None)
    result, ignored = lax.scan(scan_step, running, blocks)
    return result

def target_rows_of(points):
    return jnp.concatenate([points, jnp.ones_like(points[0])[None], lax.optimization_barrier(jnp.sum(points * points, axis=0))[None]], axis=0)

def combine(points, vortex, first, second):
    sum_kernel = first[0:3]
    velocity = cross_product(sum_kernel, points) - first[3:6]
    term_one = cross_product(sum_kernel, vortex)
    moment_one = second[6:15].reshape(3, 3, -1)
    moment_two = second[15:24].reshape(3, 3, -1)
    dot_self = lax.optimization_barrier(jnp.sum(vortex * points, axis=0))
    mixed_one = lax.optimization_barrier(jnp.sum(vortex[:, None, :] * moment_one, axis=0))
    mixed_two = lax.optimization_barrier(jnp.sum(vortex[:, None, :] * moment_two, axis=0))
    term_two = dot_self * (cross_product(second[0:3], points) - second[3:6]) - cross_product(mixed_one, points) + mixed_two
    return (velocity, term_one + term_two)

def spline_weight(distance):
    return jnp.where(distance < 1.0, 1.0 - 2.5 * distance * distance + 1.5 * distance * distance * distance, 0.5 * (2.0 - distance) * (2.0 - distance) * (1.0 - distance))

def grid_place(cell_fraction, cell_index, velocity):
    cell_start = jnp.stack([cell_index % 8, cell_index // 8 % 4, cell_index // 32]).astype(jnp.float32)
    coords = cell_start + cell_fraction + move_scale * velocity
    lowest = jnp.floor(coords)
    fraction = coords - lowest
    lowest_int = lowest.astype(jnp.int32)
    base_code = lowest_int[2] % 4 * 32 + lowest_int[1] % 4 * 8 + lowest_int[0] % 8
    return (fraction, base_code)

def node_weights(fraction):
    per_axis = [[spline_weight(fraction[axis_id] + 1.0), spline_weight(fraction[axis_id]), spline_weight(1.0 - fraction[axis_id]), spline_weight(2.0 - fraction[axis_id])] for axis_id in range(3)]
    weights = []
    for along_z in range(4):
        for along_y in range(4):
            for along_x in range(4):
                weights.append(per_axis[2][along_z] * per_axis[1][along_y] * per_axis[0][along_x])
    return jnp.stack(weights)

def cells_of(base_code):
    base_x = base_code % 8
    base_y = base_code // 8 % 4
    base_z = base_code // 32
    stencil_cells = []
    for along_z in range(4):
        for along_y in range(4):
            for along_x in range(4):
                stencil_cells.append((base_z + along_z - 1) % 4 * 32 + (base_y + along_y - 1) % 4 * 8 + (base_x + along_x - 1) % 8)
    return jnp.stack(stencil_cells)

def spread(weights, stencil_cells):
    cell_ids = jnp.arange(128, dtype=jnp.int32)[:, None]
    overall = jnp.zeros((128, weights.shape[1]), jnp.float32)
    for node in range(64):
        overall = overall + jnp.where(stencil_cells[node][None, :] == cell_ids, weights[node][None, :], 0.0)
    return overall

def reference(positions, strength, core_radius, dye_amount, cell_fraction, cell_index, tile_local, owner_dom):
    sources = jnp.concatenate([positions, strength, core_radius[None]], axis=0)
    regions = sources.reshape(7, N_DOM, REGION).transpose(1, 0, 2)

    def region_work(region_rows):
        points = region_rows[0:3]
        vortex = region_rows[3:6]
        start_sums = (jnp.zeros((6, REGION), jnp.float32), jnp.zeros((24, REGION), jnp.float32))
        first, second = block_fold(start_sums, region_rows, target_rows_of(points))
        return combine(points, vortex, first, second)
    velocity_parts, stretch_parts = lax.map(region_work, regions)
    velocity = velocity_parts.transpose(1, 0, 2).reshape(3, P_SIZE)
    stretch = stretch_parts.transpose(1, 0, 2).reshape(3, P_SIZE)
    new_strength = strength + time_step * stretch
    fraction, base_code = grid_place(cell_fraction, cell_index, velocity)
    block_owner = jnp.arange(P_SIZE, dtype=jnp.int32) // PD % N_BLK
    tile_id = ((owner_dom[:, 0] * N_BLK + block_owner) * TPD + tile_local).astype(jnp.int32)
    values = jnp.concatenate([new_strength, dye_amount[None]], axis=0)
    span = math.gcd(P_SIZE, 16384)
    pieces = P_SIZE // span
    stacked = (values.reshape(4, pieces, span).transpose(1, 0, 2), fraction.reshape(3, pieces, span).transpose(1, 0, 2), base_code.reshape(pieces, span), tile_id.reshape(pieces, span))

    def deposit_step(tile_sums, piece_rows):
        piece_values, piece_fraction, piece_base, piece_tiles = piece_rows
        spread_w = spread(node_weights(piece_fraction), cells_of(piece_base))
        contrib = jnp.einsum('cp,kp->pck', piece_values, spread_w).reshape(-1, 512)
        return (tile_sums + jax.ops.segment_sum(contrib, piece_tiles, num_segments=TILES), None)
    tile_sums, ignored = lax.scan(deposit_step, jnp.zeros((TILES, 512), jnp.float32), stacked)
    tile_grid = (tile_sums * inverse_volume).reshape(TILES, 4, 128)
    return (velocity, tile_grid)
```

```python
import functools
import math

import jax
import jax.numpy as jnp
from jax import lax
from jax.experimental import pallas as pl
from jax.experimental.pallas import tpu as pltpu
from jax.sharding import PartitionSpec as P

time_step = 0.02
move_scale = 2.0
inverse_volume = 32.0
kernel_scale = 1.0 / (4.0 * math.pi)
f32 = jnp.float32
bf16 = jnp.bfloat16
transposed_rhs = (((1,), (1,)), ((), ()))


def split3(x):
    high = x.astype(bf16).astype(f32)
    rest = x - high
    middle = rest.astype(bf16).astype(f32)
    return high, middle, rest - middle


def rows_of(array, first, count):
    return [array[first + d : first + d + 1] for d in range(count)]


def cross_rows(left, right):
    return [
        left[1] * right[2] - left[2] * right[1],
        left[2] * right[0] - left[0] * right[2],
        left[0] * right[1] - left[1] * right[0],
    ]


def square_sum(rows):
    return rows[0] * rows[0] + rows[1] * rows[1] + rows[2] * rows[2]


def target_features(points):
    one = jnp.ones_like(points[0])
    zero = jnp.zeros_like(one)
    stack = jnp.concatenate(points + [one, square_sum(points), zero, zero, zero], axis=0)
    high, middle, low = split3(stack)
    return jnp.concatenate([high, middle, high, low, high, middle], axis=0)


def source_features(src):
    points = rows_of(src, 0, 3)
    vortex = rows_of(src, 3, 3)
    radius = src[6:7]
    offset = square_sum(points) + radius * radius
    one = jnp.ones_like(radius)
    zero = jnp.zeros_like(radius)
    stack = jnp.concatenate([-2.0 * p for p in points] + [offset, one, zero, zero, zero], axis=0)
    high, middle, low = split3(stack)
    features = jnp.concatenate([high, high, middle, high, low, middle], axis=0)
    base = jnp.concatenate(vortex + cross_rows(vortex, points) + [zero, zero], axis=0)
    groups = jnp.concatenate([base] + [base * p for p in points] + [base * offset], axis=0)
    parts = split3(groups)
    moments = jnp.concatenate(list(parts) + [jnp.zeros_like(base)], axis=0)
    return features.astype(bf16), moments.astype(bf16)


def add_pair_sums(count, width, target_ref, feature_ref, moment_ref, sum_ref):
    def step(k, carry):
        start = pl.multiple_of(k * width, width)
        square = jnp.dot(
            target_ref[...], feature_ref[:, pl.ds(start, width)], preferred_element_type=f32
        )
        inverse = lax.rsqrt(square)
        inverse2 = inverse * inverse
        slope = inverse2 * inverse2 * inverse
        high = slope.astype(bf16)
        low = (slope - high.astype(f32)).astype(bf16)
        moments = moment_ref[:, pl.ds(start, width)]
        sum_ref[...] += lax.dot_general(
            high, moments, transposed_rhs, preferred_element_type=f32
        ) + lax.dot_general(low, moments, transposed_rhs, preferred_element_type=f32)
        return carry

    lax.fori_loop(0, count // width, step, 0)


def own_kernel(width, pos_ref, src_ref, sum_ref, target_ref, feature_ref, moment_ref):
    target_ref[...] = target_features(rows_of(pos_ref[...], 0, 3)).T.astype(bf16)
    features, moments = source_features(src_ref[...])
    feature_ref[...] = features
    moment_ref[...] = moments
    sum_ref[...] = jnp.zeros_like(sum_ref)
    add_pair_sums(src_ref.shape[1], width, target_ref, feature_ref, moment_ref, sum_ref)


def combine(points, vortex, sums):
    plain, by_x, by_y, by_z, by_offset = [sums[8 * k : 8 * k + 8] for k in range(5)]
    kernel = (
        square_sum(points) * plain
        + by_offset
        - 2.0 * (points[0] * by_x + points[1] * by_y + points[2] * by_z)
    ) * kernel_scale
    along = points[0] * vortex[0] + points[1] * vortex[1] + points[2] * vortex[2]
    slope = (along * plain - vortex[0] * by_x - vortex[1] * by_y - vortex[2] * by_z) * (
        -3.0 * kernel_scale
    )
    kernel_a = rows_of(kernel, 0, 3)
    velocity = [u - v for u, v in zip(cross_rows(kernel_a, points), rows_of(kernel, 3, 3))]
    term_one = cross_rows(kernel_a, vortex)
    slope_a = rows_of(slope, 0, 3)
    term_two = [u - v for u, v in zip(cross_rows(slope_a, points), rows_of(slope, 3, 3))]
    return velocity, [u + v for u, v in zip(term_one, term_two)]


def axis_weights(node, base, fraction, cells):
    t = fraction
    s = 1.0 - t
    inner = [1.0 - 2.5 * u * u + 1.5 * u * u * u for u in (t, s)]
    weights = [-0.5 * s * s * t, inner[0], inner[1], -0.5 * t * t * s]
    place = (node - base + 1) & (cells - 1)
    out = jnp.zeros(node.shape, f32)
    for k in range(4):
        out = jnp.where(place == k, weights[k], out)
    return out


def tail_kernel(
    width,
    tiles,
    owners,
    pos_ref,
    src_ref,
    before_ref,
    dye_ref,
    frac_ref,
    cell_ref,
    tile_ref,
    owner_ref,
    *refs,
):
    other_refs = refs[:-6]
    velocity_ref, grid_ref, target_ref, feature_ref, moment_ref, sum_ref = refs[-6:]
    count = src_ref.shape[1]
    points = rows_of(pos_ref[...], 0, 3)
    target_ref[...] = target_features(points).T.astype(bf16)
    for k, other_ref in enumerate(other_refs):
        features, moments = source_features(other_ref[...])
        feature_ref[:, k * count : (k + 1) * count] = features
        moment_ref[:, k * count : (k + 1) * count] = moments
    sum_ref[...] = before_ref[...]
    add_pair_sums(
        len(other_refs) * count, width, target_ref, feature_ref, moment_ref, sum_ref
    )
    sums = sum_ref[...].T
    sums = sums[0:40] + sums[40:80] + sums[80:120]
    vortex = rows_of(src_ref[...], 3, 3)
    velocity, stretch = combine(points, vortex, sums)
    velocity_ref[...] = jnp.concatenate(velocity, axis=0)

    values = [inverse_volume * (a + time_step * d) for a, d in zip(vortex, stretch)]
    values.append(inverse_volume * dye_ref[...])
    cell = cell_ref[...]
    starts = [cell & 7, (cell >> 3) & 3, cell >> 5]
    bases, fractions = [], []
    for d in range(3):
        place = starts[d].astype(f32) + frac_ref[d : d + 1, :] + move_scale * velocity[d]
        lowest = jnp.floor(place)
        bases.append(lowest.astype(jnp.int32))
        fractions.append(place - lowest)
    node = lax.broadcasted_iota(jnp.int32, (8, count), 0)
    weight_x = axis_weights(node, bases[0], fractions[0], 8)
    node = lax.broadcasted_iota(jnp.int32, (16, count), 0)
    weight_zy = axis_weights(node & 3, bases[1], fractions[1], 4) * axis_weights(
        node >> 2, bases[2], fractions[2], 4
    )
    spread = jnp.concatenate([weight_zy[k : k + 1] * weight_x for k in range(16)], axis=0)
    spread_high = spread.astype(bf16)
    spread_low = (spread - spread_high.astype(f32)).astype(bf16)
    spread_both = jnp.concatenate([spread_high, spread_low], axis=0)

    me = lax.axis_index("dom")
    slot = owner_ref[...] ^ me
    node = lax.broadcasted_iota(jnp.int32, (16, count), 0)
    mine = slot * tiles + tile_ref[...] - (node >> 2)
    value = jnp.concatenate(values * 4, axis=0)
    value_high = value.astype(bf16).astype(f32)
    value_low = value - value_high
    half = 8
    per_group = tiles // half * half // 4
    for group in range(owners * tiles // (4 * half)):
        masks = [mine == 4 * (group * half + k) for k in range(half)]
        picked_high = jnp.concatenate(
            [jnp.where(m, value_high, 0.0).astype(bf16) for m in masks], axis=0
        )
        picked_low = jnp.concatenate(
            [jnp.where(m, value_low, 0.0).astype(bf16) for m in masks], axis=0
        )
        both = lax.dot_general(
            picked_high, spread_both, transposed_rhs, preferred_element_type=f32
        )
        low = lax.dot_general(
            picked_low, spread_high, transposed_rhs, preferred_element_type=f32
        )
        grid_ref[group * 16 * half : (group + 1) * 16 * half, :] = (
            both[:, 0:128] + both[:, 128:256] + low
        )


def vmem_specs(count):
    return [pl.BlockSpec(memory_space=pltpu.VMEM)] * count


def on_device(
    positions, strength, core_radius, dye_amount, cell_fraction, cell_index, tile_local, owner_dom
):
    count = positions.shape[1]
    tiles = count // 128
    owners = lax.axis_size("dom")
    blocks = lax.axis_size("blk")
    width = math.gcd(count, 512)
    sources = jnp.concatenate([positions, strength, core_radius[None]], axis=0)
    others = [
        lax.ppermute(sources, "blk", [(i, (i + s) % blocks) for i in range(blocks)])
        for s in range(1, blocks)
    ]
    scratch = lambda n: [
        pltpu.VMEM((count, 48), bf16),
        pltpu.VMEM((48, n * count), bf16),
        pltpu.VMEM((128, n * count), bf16),
    ]
    params = pltpu.CompilerParams(vmem_limit_bytes=48 * 2**20)
    cost = lambda n: pl.CostEstimate(
        flops=n * count * count * 256 * 2 * 3,
        bytes_accessed=4 * count * 256,
        transcendentals=n * count * count,
    )
    own_sums = pl.pallas_call(
        functools.partial(own_kernel, width),
        out_shape=jax.ShapeDtypeStruct((count, 128), f32),
        in_specs=vmem_specs(2),
        out_specs=vmem_specs(1)[0],
        scratch_shapes=scratch(1),
        compiler_params=params,
        cost_estimate=cost(1),
        name="own_pairs",
    )(positions, sources)
    velocity, grid = pl.pallas_call(
        functools.partial(tail_kernel, width, tiles, owners),
        out_shape=(
            jax.ShapeDtypeStruct((3, count), f32),
            jax.ShapeDtypeStruct((owners * tiles * 4, 128), f32),
        ),
        in_specs=vmem_specs(8 + len(others)),
        out_specs=tuple(vmem_specs(2)),
        scratch_shapes=scratch(len(others)) + [pltpu.VMEM((count, 128), f32)],
        compiler_params=params,
        cost_estimate=cost(len(others)),
        name="other_pairs_and_deposit",
    )(
        positions,
        sources,
        own_sums,
        dye_amount[None],
        cell_fraction,
        cell_index[None],
        tile_local[None],
        owner_dom.reshape(1, count),
        *others,
    )
    step = owners // 2
    grid = grid.reshape(owners, tiles * 4, 128)
    bit = 1
    while bit < owners:
        pairs = grid.reshape(-1, 2, *grid.shape[1:])
        got = lax.ppermute(pairs[:, 1], "dom", [(i, i ^ bit) for i in range(owners)])
        grid = pairs[:, 0] + got
        bit *= 2
    return velocity, grid.reshape(tiles, 4, 128)


def solution(mesh):
    both = ("dom", "blk")
    placed = (
        P(None, both),
        P(None, both),
        P(both),
        P(both),
        P(None, both),
        P(both),
        P(both),
        P(both, None),
    )
    return jax.shard_map(
        on_device,
        mesh=mesh,
        in_specs=placed,
        out_specs=(P(None, both), P(both, None, None)),
        check_vma=False,
    )
```

```python
import functools
import math

import jax
import jax.numpy as jnp
from jax import lax
from jax.experimental import pallas as pl
from jax.experimental.pallas import tpu as pltpu
from jax.sharding import PartitionSpec as P

time_step = 0.02
move_scale = 2.0
inverse_volume = 32.0
kernel_scale = 1.0 / (4.0 * math.pi)
f32 = jnp.float32
bf16 = jnp.bfloat16
transposed_rhs = (((1,), (1,)), ((), ()))


def split3(x):
    high = x.astype(bf16).astype(f32)
    rest = x - high
    middle = rest.astype(bf16).astype(f32)
    return high, middle, rest - middle


def rows_of(array, first, count):
    return [array[first + d : first + d + 1] for d in range(count)]


def cross_rows(left, right):
    return [
        left[1] * right[2] - left[2] * right[1],
        left[2] * right[0] - left[0] * right[2],
        left[0] * right[1] - left[1] * right[0],
    ]


def square_sum(rows):
    return rows[0] * rows[0] + rows[1] * rows[1] + rows[2] * rows[2]


def target_features(points):
    one = jnp.ones_like(points[0])
    zero = jnp.zeros_like(one)
    stack = jnp.concatenate(points + [one, square_sum(points), zero, zero, zero], axis=0)
    high, middle, low = split3(stack)
    return jnp.concatenate([high, middle, high, low, high, middle], axis=0)


def source_features(src):
    points = rows_of(src, 0, 3)
    vortex = rows_of(src, 3, 3)
    radius = src[6:7]
    offset = square_sum(points) + radius * radius
    one = jnp.ones_like(radius)
    zero = jnp.zeros_like(radius)
    stack = jnp.concatenate([-2.0 * p for p in points] + [offset, one, zero, zero, zero], axis=0)
    high, middle, low = split3(stack)
    features = jnp.concatenate([high, high, middle, high, low, middle], axis=0)
    base = jnp.concatenate(vortex + cross_rows(vortex, points) + [zero, zero], axis=0)
    groups = jnp.concatenate([base] + [base * p for p in points] + [base * offset], axis=0)
    moments = jnp.concatenate(list(split3(groups)) + [jnp.zeros_like(base)], axis=0)
    return features.astype(bf16), moments.astype(bf16)


def add_pair_sums(count, target_ref, feature_ref, moment_ref, sum_ref, slope_ref):
    targets = sum_ref.shape[0]
    width = slope_ref.shape[1]
    chunk = math.gcd(targets, 256)
    chunks = targets // chunk
    lag = min(2, chunks)

    def produce(start, number):
        rows = slice(number * chunk, (number + 1) * chunk)
        square = jnp.dot(
            target_ref[rows, :], feature_ref[:, pl.ds(start, width)], preferred_element_type=f32
        )
        inverse = lax.rsqrt(square)
        inverse2 = inverse * inverse
        slope = inverse2 * inverse2 * inverse
        high = slope.astype(bf16)
        first = 2 * number * chunk
        slope_ref[first : first + chunk, :] = high
        slope_ref[first + chunk : first + 2 * chunk, :] = (slope - high.astype(f32)).astype(bf16)

    def consume(start, number):
        both = lax.dot_general(
            slope_ref[2 * number * chunk : 2 * (number + 1) * chunk, :],
            moment_ref[:, pl.ds(start, width)],
            transposed_rhs,
            preferred_element_type=f32,
        )
        sum_ref[number * chunk : (number + 1) * chunk, :] += both[:chunk] + both[chunk:]

    first = 2 * (chunks - lag) * chunk
    slope_ref[first:, :] = jnp.zeros((2 * lag * chunk, width), bf16)
    steps = count // width
    unroll = math.gcd(steps, 4)

    def step(k, carry):
        for u in range(unroll):
            start = pl.multiple_of((k * unroll + u) * width, width)
            before = pl.multiple_of(jnp.maximum(k * unroll + u - 1, 0) * width, width)
            for number in range(chunks):
                if number >= lag:
                    consume(start, number - lag)
                else:
                    consume(before, number - lag + chunks)
                produce(start, number)
        return carry

    lax.fori_loop(0, steps // unroll, step, 0)
    for number in range(chunks - lag, chunks):
        consume((steps - 1) * width, number)


def own_kernel(
    pos_ref, src_ref, sum_ref, target_ref, feature_ref, moment_ref, slope_ref
):
    target_ref[...] = target_features(rows_of(pos_ref[...], 0, 3)).T.astype(bf16)
    feature_ref[...], moment_ref[...] = source_features(src_ref[...])
    sum_ref[...] = jnp.zeros_like(sum_ref)
    add_pair_sums(
        src_ref.shape[1],
        target_ref,
        feature_ref,
        moment_ref,
        sum_ref,
        slope_ref,
    )


def combine(points, vortex, sums):
    plain, by_x, by_y, by_z, by_offset = [sums[8 * k : 8 * k + 8] for k in range(5)]
    kernel = (
        square_sum(points) * plain
        + by_offset
        - 2.0 * (points[0] * by_x + points[1] * by_y + points[2] * by_z)
    ) * kernel_scale
    along = points[0] * vortex[0] + points[1] * vortex[1] + points[2] * vortex[2]
    slope = (along * plain - vortex[0] * by_x - vortex[1] * by_y - vortex[2] * by_z) * (
        -3.0 * kernel_scale
    )
    kernel_a = rows_of(kernel, 0, 3)
    velocity = [u - v for u, v in zip(cross_rows(kernel_a, points), rows_of(kernel, 3, 3))]
    term_one = cross_rows(kernel_a, vortex)
    slope_a = rows_of(slope, 0, 3)
    term_two = [u - v for u, v in zip(cross_rows(slope_a, points), rows_of(slope, 3, 3))]
    return velocity, [u + v for u, v in zip(term_one, term_two)]


def axis_weights(node, base, fraction, cells):
    t = fraction
    s = 1.0 - t
    inner = [1.0 - 2.5 * u * u + 1.5 * u * u * u for u in (t, s)]
    weights = [-0.5 * s * s * t, inner[0], inner[1], -0.5 * t * t * s]
    place = (node - base + 1) & (cells - 1)
    out = jnp.zeros(node.shape, f32)
    for k in range(4):
        out = jnp.where(place == k, weights[k], out)
    return out


def tail_kernel(
    tiles,
    owners,
    pos_ref,
    src_ref,
    before_ref,
    dye_ref,
    frac_ref,
    cell_ref,
    tile_ref,
    owner_ref,
    *refs,
):
    other_refs = refs[:-9]
    velocity_ref, keep_ref, send_ref, *refs = refs[-9:]
    target_ref, feature_ref, moment_ref, slope_ref, sum_ref, pick_ref = refs
    count = src_ref.shape[1]
    points = rows_of(pos_ref[...], 0, 3)
    target_ref[...] = target_features(points).T.astype(bf16)
    for k, other_ref in enumerate(other_refs):
        place = slice(k * count, (k + 1) * count)
        feature_ref[:, place], moment_ref[:, place] = source_features(other_ref[...])
    sum_ref[...] = before_ref[...]
    add_pair_sums(
        len(other_refs) * count,
        target_ref,
        feature_ref,
        moment_ref,
        sum_ref,
        slope_ref,
    )
    sums = sum_ref[...].T
    sums = sums[0:40] + sums[40:80] + sums[80:120]
    vortex = rows_of(src_ref[...], 3, 3)
    velocity, stretch = combine(points, vortex, sums)
    velocity_ref[...] = jnp.concatenate(velocity, axis=0)

    values = [inverse_volume * (a + time_step * d) for a, d in zip(vortex, stretch)]
    values.append(inverse_volume * dye_ref[...])
    cell = cell_ref[...]
    starts = [cell & 7, (cell >> 3) & 3, cell >> 5]
    bases, fractions = [], []
    for d in range(3):
        place = starts[d].astype(f32) + frac_ref[d : d + 1, :] + move_scale * velocity[d]
        lowest = jnp.floor(place)
        bases.append(lowest.astype(jnp.int32))
        fractions.append(place - lowest)
    node = lax.broadcasted_iota(jnp.int32, (8, count), 0)
    weight_x = axis_weights(node, bases[0], fractions[0], 8)
    node = lax.broadcasted_iota(jnp.int32, (16, count), 0)
    weight_zy = axis_weights(node & 3, bases[1], fractions[1], 4) * axis_weights(
        node >> 2, bases[2], fractions[2], 4
    )
    spread = jnp.concatenate([weight_zy[k : k + 1] * weight_x for k in range(16)], axis=0)
    spread_high = spread.astype(bf16)
    spread_low = (spread - spread_high.astype(f32)).astype(bf16)
    spread_both = jnp.concatenate([spread_high, spread_low], axis=0)

    slot = owner_ref[...] ^ lax.axis_index("dom")
    slot = (slot & 1) * (owners // 2) + (slot >> 1)
    node = lax.broadcasted_iota(jnp.int32, (16, count), 0)
    mine = slot * tiles + tile_ref[...] - (node >> 2)
    value = jnp.concatenate(values * 4, axis=0)
    value_high = value.astype(bf16).astype(f32)
    value_low = value - value_high
    total = owners * tiles * 4
    for group in range(total // 16):
        mask = mine == 4 * group
        first = 16 * group
        pick_ref[first : first + 16, :] = jnp.where(mask, value_high, 0.0).astype(bf16)
        first = total + 16 * group
        pick_ref[first : first + 16, :] = jnp.where(mask, value_low, 0.0).astype(bf16)
    both = lax.dot_general(
        pick_ref[...], spread_both, transposed_rhs, preferred_element_type=f32
    )
    both = both[:, 0:128] + both[:, 128:256]
    both = both[:total] + both[total:]
    keep_ref[...] = both[: total // 2]
    send_ref[...] = both[total // 2 :]


def vmem_specs(count):
    return [pl.BlockSpec(memory_space=pltpu.VMEM)] * count


def on_device(
    positions, strength, core_radius, dye_amount, cell_fraction, cell_index, tile_local, owner_dom
):
    count = positions.shape[1]
    tiles = count // 128
    owners = lax.axis_size("dom")
    blocks = lax.axis_size("blk")
    width = math.gcd(count, 512)
    sources = jnp.concatenate([positions, strength, core_radius[None]], axis=0)
    others = [
        lax.ppermute(sources, "blk", [(i, (i + s) % blocks) for i in range(blocks)])
        for s in range(1, blocks)
    ]
    scratch = lambda n: [
        pltpu.VMEM((count, 48), bf16),
        pltpu.VMEM((48, n * count), bf16),
        pltpu.VMEM((128, n * count), bf16),
        pltpu.VMEM((2 * count, width), bf16),
    ]
    params = pltpu.CompilerParams(vmem_limit_bytes=48 * 2**20)
    cost = lambda n: pl.CostEstimate(
        flops=n * count * count * 256 * 2 * 3,
        bytes_accessed=4 * count * 256,
        transcendentals=n * count * count,
    )
    own_sums = pl.pallas_call(
        own_kernel,
        out_shape=jax.ShapeDtypeStruct((count, 128), f32),
        in_specs=vmem_specs(2),
        out_specs=vmem_specs(1)[0],
        scratch_shapes=scratch(1),
        compiler_params=params,
        cost_estimate=cost(1),
        name="own_pairs",
    )(positions, sources)
    half = jax.ShapeDtypeStruct((owners * tiles * 2, 128), f32)
    velocity, keep, send = pl.pallas_call(
        functools.partial(tail_kernel, tiles, owners),
        out_shape=(jax.ShapeDtypeStruct((3, count), f32), half, half),
        in_specs=vmem_specs(8 + len(others)),
        out_specs=tuple(vmem_specs(3)),
        scratch_shapes=scratch(len(others))
        + [pltpu.VMEM((count, 128), f32), pltpu.VMEM((owners * tiles * 8, count), bf16)],
        compiler_params=params,
        cost_estimate=cost(len(others)),
        name="other_pairs_and_deposit",
    )(
        positions,
        sources,
        own_sums,
        dye_amount[None],
        cell_fraction,
        cell_index[None],
        tile_local[None],
        owner_dom.reshape(1, count),
        *others,
    )
    exchange = lambda x, s: lax.ppermute(x, "dom", [(i, i ^ s) for i in range(owners)])
    grid = (keep + exchange(send, 1)).reshape(owners // 2, tiles, 4, 128)
    got = [exchange(grid[j], 2 * j) for j in range(owners // 2 - 1, 0, -1)]
    return velocity, sum(got, grid[0])


def solution(mesh):
    both = ("dom", "blk")
    placed = (
        P(None, both),
        P(None, both),
        P(both),
        P(both),
        P(None, both),
        P(both),
        P(both),
        P(both, None),
    )
    return jax.shard_map(
        on_device,
        mesh=mesh,
        in_specs=placed,
        out_specs=(P(None, both), P(both, None, None)),
        check_vma=False,
    )
```

```python
import functools
import math

import jax
import jax.numpy as jnp
from jax import lax
from jax.experimental import pallas as pl
from jax.experimental.pallas import tpu as pltpu
from jax.sharding import PartitionSpec as P

time_step = 0.02
move_scale = 2.0
inverse_volume = 32.0
kernel_scale = 1.0 / (4.0 * math.pi)
f32 = jnp.float32
bf16 = jnp.bfloat16
transposed_rhs = (((1,), (1,)), ((), ()))


def split3(x):
    high = x.astype(bf16).astype(f32)
    rest = x - high
    middle = rest.astype(bf16).astype(f32)
    return high, middle, rest - middle


def rows_of(array, first, count):
    return [array[first + d : first + d + 1] for d in range(count)]


def cross_rows(left, right):
    return [
        left[1] * right[2] - left[2] * right[1],
        left[2] * right[0] - left[0] * right[2],
        left[0] * right[1] - left[1] * right[0],
    ]


def square_sum(rows):
    return rows[0] * rows[0] + rows[1] * rows[1] + rows[2] * rows[2]


def target_features(points):
    one = jnp.ones_like(points[0])
    zero = jnp.zeros_like(one)
    stack = jnp.concatenate(points + [one, square_sum(points), zero, zero, zero], axis=0)
    high, middle, low = split3(stack)
    return jnp.concatenate([high, middle, high, low, high, middle], axis=0)


def source_features(src):
    points = rows_of(src, 0, 3)
    vortex = rows_of(src, 3, 3)
    radius = src[6:7]
    offset = square_sum(points) + radius * radius
    one = jnp.ones_like(radius)
    zero = jnp.zeros_like(radius)
    stack = jnp.concatenate([-2.0 * p for p in points] + [offset, one, zero, zero, zero], axis=0)
    high, middle, low = split3(stack)
    features = jnp.concatenate([high, high, middle, high, low, middle], axis=0)
    base = jnp.concatenate(vortex + cross_rows(vortex, points), axis=0)
    groups = jnp.concatenate([base] + [base * p for p in points] + [base * offset], axis=0)
    moments = jnp.concatenate(list(split3(groups)) + [jnp.zeros_like(base)], axis=0)
    return features.astype(bf16), moments.astype(bf16)


def add_pair_sums(count, target_ref, feature_ref, moment_ref, sum_ref, slope_ref):
    targets = sum_ref.shape[1]
    width = slope_ref.shape[1]
    chunk = math.gcd(targets, 256)
    chunks = targets // chunk
    lag = min(4, chunks)

    def produce(start, number):
        rows = slice(number * chunk, (number + 1) * chunk)
        square = jnp.dot(
            target_ref[rows, :], feature_ref[:, pl.ds(start, width)], preferred_element_type=f32
        )
        inverse = lax.rsqrt(square)
        inverse2 = inverse * inverse
        slope = inverse2 * inverse2 * inverse
        high = slope.astype(bf16)
        first = 2 * number * chunk
        slope_ref[first : first + chunk, :] = high
        slope_ref[first + chunk : first + 2 * chunk, :] = (slope - high.astype(f32)).astype(bf16)

    def consume(start, number):
        both = lax.dot_general(
            moment_ref[:, pl.ds(start, width)],
            slope_ref[2 * number * chunk : 2 * (number + 1) * chunk, :],
            transposed_rhs,
            preferred_element_type=f32,
        )
        sum_ref[:, number * chunk : (number + 1) * chunk] += both[:, :chunk] + both[:, chunk:]

    first = 2 * (chunks - lag) * chunk
    slope_ref[first:, :] = jnp.zeros((2 * lag * chunk, width), bf16)
    steps = count // width
    unroll = math.gcd(steps, 8)

    def step(k, carry):
        for u in range(unroll):
            start = pl.multiple_of((k * unroll + u) * width, width)
            before = pl.multiple_of(jnp.maximum(k * unroll + u - 1, 0) * width, width)
            for number in range(chunks):
                if number >= lag:
                    consume(start, number - lag)
                else:
                    consume(before, number - lag + chunks)
                produce(start, number)
        return carry

    lax.fori_loop(0, steps // unroll, step, 0)
    for number in range(chunks - lag, chunks):
        consume((steps - 1) * width, number)


def own_kernel(
    pos_ref, src_ref, sum_ref, target_ref, feature_ref, moment_ref, slope_ref
):
    target_ref[...] = target_features(rows_of(pos_ref[...], 0, 3)).T.astype(bf16)
    feature_ref[...], moment_ref[...] = source_features(src_ref[...])
    sum_ref[...] = jnp.zeros_like(sum_ref)
    add_pair_sums(
        src_ref.shape[1],
        target_ref,
        feature_ref,
        moment_ref,
        sum_ref,
        slope_ref,
    )


def combine(points, vortex, sums):
    plain, by_x, by_y, by_z, by_offset = [sums[6 * k : 6 * k + 6] for k in range(5)]
    kernel = (
        square_sum(points) * plain
        + by_offset
        - 2.0 * (points[0] * by_x + points[1] * by_y + points[2] * by_z)
    ) * kernel_scale
    along = points[0] * vortex[0] + points[1] * vortex[1] + points[2] * vortex[2]
    slope = (along * plain - vortex[0] * by_x - vortex[1] * by_y - vortex[2] * by_z) * (
        -3.0 * kernel_scale
    )
    kernel_a = rows_of(kernel, 0, 3)
    velocity = [u - v for u, v in zip(cross_rows(kernel_a, points), rows_of(kernel, 3, 3))]
    term_one = cross_rows(kernel_a, vortex)
    slope_a = rows_of(slope, 0, 3)
    term_two = [u - v for u, v in zip(cross_rows(slope_a, points), rows_of(slope, 3, 3))]
    return velocity, [u + v for u, v in zip(term_one, term_two)]


def axis_weights(node, base, fraction, cells):
    t = fraction
    s = 1.0 - t
    inner = [1.0 - 2.5 * u * u + 1.5 * u * u * u for u in (t, s)]
    weights = [-0.5 * s * s * t, inner[0], inner[1], -0.5 * t * t * s]
    place = (node - base + 1) & (cells - 1)
    out = jnp.zeros(node.shape, f32)
    for k in range(4):
        out = jnp.where(place == k, weights[k], out)
    return out


def tail_kernel(
    tiles,
    owners,
    pos_ref,
    src_ref,
    before_ref,
    dye_ref,
    frac_ref,
    cell_ref,
    tile_ref,
    owner_ref,
    *refs,
):
    other_refs = refs[:-9]
    velocity_ref, keep_ref, send_ref, *refs = refs[-9:]
    target_ref, feature_ref, moment_ref, slope_ref, sum_ref, pick_ref = refs
    count = src_ref.shape[1]
    points = rows_of(pos_ref[...], 0, 3)
    target_ref[...] = target_features(points).T.astype(bf16)
    for k, other_ref in enumerate(other_refs):
        place = slice(k * count, (k + 1) * count)
        feature_ref[:, place], moment_ref[:, place] = source_features(other_ref[...])
    sum_ref[...] = before_ref[...]
    add_pair_sums(
        len(other_refs) * count,
        target_ref,
        feature_ref,
        moment_ref,
        sum_ref,
        slope_ref,
    )
    sums = sum_ref[0:30, :] + sum_ref[30:60, :] + sum_ref[60:90, :]
    vortex = rows_of(src_ref[...], 3, 3)
    velocity, stretch = combine(points, vortex, sums)
    velocity_ref[...] = jnp.concatenate(velocity, axis=0)

    values = [inverse_volume * (a + time_step * d) for a, d in zip(vortex, stretch)]
    values.append(inverse_volume * dye_ref[...])
    cell = cell_ref[...]
    starts = [cell & 7, (cell >> 3) & 3, cell >> 5]
    bases, fractions = [], []
    for d in range(3):
        place = starts[d].astype(f32) + frac_ref[d : d + 1, :] + move_scale * velocity[d]
        lowest = jnp.floor(place)
        bases.append(lowest.astype(jnp.int32))
        fractions.append(place - lowest)
    node = lax.broadcasted_iota(jnp.int32, (8, count), 0)
    weight_x = axis_weights(node, bases[0], fractions[0], 8)
    node = lax.broadcasted_iota(jnp.int32, (16, count), 0)
    weight_zy = axis_weights(node & 3, bases[1], fractions[1], 4) * axis_weights(
        node >> 2, bases[2], fractions[2], 4
    )
    spread = jnp.concatenate([weight_zy[k : k + 1] * weight_x for k in range(16)], axis=0)
    spread_high = spread.astype(bf16)
    spread_low = (spread - spread_high.astype(f32)).astype(bf16)
    spread_both = jnp.concatenate([spread_high, spread_low], axis=0)

    slot = owner_ref[...] ^ lax.axis_index("dom")
    slot = (slot & 1) * (owners // 2) + (slot >> 1)
    node = lax.broadcasted_iota(jnp.int32, (16, count), 0)
    mine = slot * tiles + tile_ref[...] - (node >> 2)
    value = jnp.concatenate(values * 4, axis=0)
    value_high = value.astype(bf16).astype(f32)
    value_low = value - value_high
    total = owners * tiles * 4
    for group in range(total // 16):
        mask = mine == 4 * group
        first = 16 * group
        pick_ref[first : first + 16, :] = jnp.where(mask, value_high, 0.0).astype(bf16)
        first = total + 16 * group
        pick_ref[first : first + 16, :] = jnp.where(mask, value_low, 0.0).astype(bf16)
    both = lax.dot_general(
        pick_ref[...], spread_both, transposed_rhs, preferred_element_type=f32
    )
    both = both[:, 0:128] + both[:, 128:256]
    both = both[:total] + both[total:]
    keep_ref[...] = both[: total // 2]
    send_ref[...] = both[total // 2 :]


def vmem_specs(count):
    return [pl.BlockSpec(memory_space=pltpu.VMEM)] * count


def on_device(
    positions, strength, core_radius, dye_amount, cell_fraction, cell_index, tile_local, owner_dom
):
    count = positions.shape[1]
    tiles = count // 128
    owners = lax.axis_size("dom")
    blocks = lax.axis_size("blk")
    width = math.gcd(count, 256)
    sources = jnp.concatenate([positions, strength, core_radius[None]], axis=0)
    others = [
        lax.ppermute(sources, "blk", [(i, (i + s) % blocks) for i in range(blocks)])
        for s in range(1, blocks)
    ]
    scratch = lambda n: [
        pltpu.VMEM((count, 48), bf16),
        pltpu.VMEM((48, n * count), bf16),
        pltpu.VMEM((96, n * count), bf16),
        pltpu.VMEM((2 * count, width), bf16),
    ]
    params = pltpu.CompilerParams(vmem_limit_bytes=48 * 2**20)
    cost = lambda n: pl.CostEstimate(
        flops=n * count * count * 256 * 2 * 3,
        bytes_accessed=4 * count * 256,
        transcendentals=n * count * count,
    )
    own_sums = pl.pallas_call(
        own_kernel,
        out_shape=jax.ShapeDtypeStruct((96, count), f32),
        in_specs=vmem_specs(2),
        out_specs=vmem_specs(1)[0],
        scratch_shapes=scratch(1),
        compiler_params=params,
        cost_estimate=cost(1),
        name="own_pairs",
    )(positions, sources)
    half = jax.ShapeDtypeStruct((owners * tiles * 2, 128), f32)
    velocity, keep, send = pl.pallas_call(
        functools.partial(tail_kernel, tiles, owners),
        out_shape=(jax.ShapeDtypeStruct((3, count), f32), half, half),
        in_specs=vmem_specs(8 + len(others)),
        out_specs=tuple(vmem_specs(3)),
        scratch_shapes=scratch(len(others))
        + [pltpu.VMEM((96, count), f32), pltpu.VMEM((owners * tiles * 8, count), bf16)],
        compiler_params=params,
        cost_estimate=cost(len(others)),
        name="other_pairs_and_deposit",
    )(
        positions,
        sources,
        own_sums,
        dye_amount[None],
        cell_fraction,
        cell_index[None],
        tile_local[None],
        owner_dom.reshape(1, count),
        *others,
    )
    exchange = lambda x, s: lax.ppermute(x, "dom", [(i, i ^ s) for i in range(owners)])
    grid = (keep + exchange(send, 1)).reshape(owners // 2, tiles, 4, 128)
    got = [exchange(grid[j], 2 * j) for j in range(owners // 2 - 1, 0, -1)]
    return velocity, sum(got, grid[0])


def solution(mesh):
    both = ("dom", "blk")
    placed = (
        P(None, both),
        P(None, both),
        P(both),
        P(both),
        P(None, both),
        P(both),
        P(both),
        P(both, None),
    )
    return jax.shard_map(
        on_device,
        mesh=mesh,
        in_specs=placed,
        out_specs=(P(None, both), P(both, None, None)),
        check_vma=False,
    )
```

```python
import functools
import math

import jax
import jax.numpy as jnp
from jax import lax
from jax.experimental import pallas as pl
from jax.experimental.pallas import tpu as pltpu
from jax.sharding import PartitionSpec as P

time_step = 0.02
move_scale = 2.0
inverse_volume = 32.0
kernel_scale = 1.0 / (4.0 * math.pi)
f32 = jnp.float32
bf16 = jnp.bfloat16
transposed_rhs = (((1,), (1,)), ((), ()))


def split3(x):
    high = x.astype(bf16).astype(f32)
    rest = x - high
    middle = rest.astype(bf16).astype(f32)
    return high, middle, rest - middle


def rows_of(array, first, count):
    return [array[first + d : first + d + 1] for d in range(count)]


def cross_rows(left, right):
    return [
        left[1] * right[2] - left[2] * right[1],
        left[2] * right[0] - left[0] * right[2],
        left[0] * right[1] - left[1] * right[0],
    ]


def square_sum(rows):
    return rows[0] * rows[0] + rows[1] * rows[1] + rows[2] * rows[2]


def target_features(points):
    one = jnp.ones_like(points[0])
    zero = jnp.zeros_like(one)
    stack = jnp.concatenate(points + [one, square_sum(points), zero, zero, zero], axis=0)
    high, middle, low = split3(stack)
    return jnp.concatenate([high, middle, high, low, high, middle], axis=0)


def source_features(src):
    points = rows_of(src, 0, 3)
    vortex = rows_of(src, 3, 3)
    radius = src[6:7]
    offset = square_sum(points) + radius * radius
    one = jnp.ones_like(radius)
    zero = jnp.zeros_like(radius)
    stack = jnp.concatenate([-2.0 * p for p in points] + [offset, one, zero, zero, zero], axis=0)
    high, middle, low = split3(stack)
    features = jnp.concatenate([high, high, middle, high, low, middle], axis=0)
    base = jnp.concatenate(vortex + cross_rows(vortex, points), axis=0)
    groups = jnp.concatenate([base] + [base * p for p in points] + [base * offset], axis=0)
    moments = jnp.concatenate(list(split3(groups)) + [jnp.zeros_like(base)], axis=0)
    return features.T.astype(bf16), moments.astype(bf16)


def add_pair_sums(lag, unroll, target_ref, feature_ref, moment_ref, sum_ref, slope_ref):
    targets = sum_ref.shape[1]
    slots, chunk, width = slope_ref.shape
    chunk = chunk // 2
    chunks = feature_ref.shape[0] // chunk
    tiles = targets // width
    lag = min(lag, chunks)

    def produce(start, number):
        square = jnp.dot(
            feature_ref[number * chunk : (number + 1) * chunk, :],
            target_ref[:, pl.ds(start, width)],
            preferred_element_type=f32,
        )
        inverse = lax.rsqrt(square)
        inverse2 = inverse * inverse
        slope = inverse2 * inverse2 * inverse
        high = slope.astype(bf16)
        slope_ref[number % slots, :chunk] = high
        slope_ref[number % slots, chunk:] = (slope - high.astype(f32)).astype(bf16)

    def consume(start, number):
        moments = moment_ref[:, number * chunk : (number + 1) * chunk]
        sum_ref[:, pl.ds(start, width)] += jnp.dot(
            moments, slope_ref[number % slots, :chunk], preferred_element_type=f32
        ) + jnp.dot(moments, slope_ref[number % slots, chunk:], preferred_element_type=f32)

    for number in range(chunks - lag, chunks):
        slope_ref[number % slots] = jnp.zeros(slope_ref.shape[1:], bf16)

    def step(k, carry):
        for u in range(unroll):
            start = pl.multiple_of((k * unroll + u) * width, width)
            before = pl.multiple_of(jnp.maximum(k * unroll + u - 1, 0) * width, width)
            for number in range(chunks):
                if number >= lag:
                    consume(start, number - lag)
                else:
                    consume(before, number - lag + chunks)
                produce(start, number)
        return carry

    lax.fori_loop(0, tiles // unroll, step, 0)
    for number in range(chunks - lag, chunks):
        consume((tiles - 1) * width, number)


def own_kernel(
    pos_ref, src_ref, sum_ref, target_ref, feature_ref, moment_ref, slope_ref
):
    target_ref[...] = target_features(rows_of(pos_ref[...], 0, 3)).astype(bf16)
    feature_ref[...], moment_ref[...] = source_features(src_ref[...])
    sum_ref[...] = jnp.zeros_like(sum_ref)
    tiles = sum_ref.shape[1] // slope_ref.shape[2]
    add_pair_sums(
        4, math.gcd(tiles, 8), target_ref, feature_ref, moment_ref, sum_ref, slope_ref
    )


def combine(points, vortex, sums):
    plain, by_x, by_y, by_z, by_offset = [sums[6 * k : 6 * k + 6] for k in range(5)]
    kernel = (
        square_sum(points) * plain
        + by_offset
        - 2.0 * (points[0] * by_x + points[1] * by_y + points[2] * by_z)
    ) * kernel_scale
    along = points[0] * vortex[0] + points[1] * vortex[1] + points[2] * vortex[2]
    slope = (along * plain - vortex[0] * by_x - vortex[1] * by_y - vortex[2] * by_z) * (
        -3.0 * kernel_scale
    )
    kernel_a = rows_of(kernel, 0, 3)
    velocity = [u - v for u, v in zip(cross_rows(kernel_a, points), rows_of(kernel, 3, 3))]
    term_one = cross_rows(kernel_a, vortex)
    slope_a = rows_of(slope, 0, 3)
    term_two = [u - v for u, v in zip(cross_rows(slope_a, points), rows_of(slope, 3, 3))]
    return velocity, [u + v for u, v in zip(term_one, term_two)]


def axis_weights(node, base, fraction, cells):
    t = fraction
    s = 1.0 - t
    inner = [1.0 - 2.5 * u * u + 1.5 * u * u * u for u in (t, s)]
    weights = [-0.5 * s * s * t, inner[0], inner[1], -0.5 * t * t * s]
    place = (node - base + 1) & (cells - 1)
    out = jnp.zeros(node.shape, f32)
    for k in range(4):
        out = jnp.where(place == k, weights[k], out)
    return out


def tail_kernel(
    tiles,
    owners,
    pos_ref,
    src_ref,
    before_ref,
    dye_ref,
    frac_ref,
    cell_ref,
    tile_ref,
    owner_ref,
    *refs,
):
    other_refs = refs[:-9]
    velocity_ref, keep_ref, send_ref, *refs = refs[-9:]
    target_ref, feature_ref, moment_ref, slope_ref, sum_ref, pick_ref = refs
    count = src_ref.shape[1]
    points = rows_of(pos_ref[...], 0, 3)
    target_ref[...] = target_features(points).astype(bf16)
    for k, other_ref in enumerate(other_refs):
        place = slice(k * count, (k + 1) * count)
        feature_ref[place], moment_ref[:, place] = source_features(other_ref[...])
    sum_ref[...] = before_ref[...]
    add_pair_sums(
        8,
        math.gcd(count // slope_ref.shape[2], 2),
        target_ref,
        feature_ref,
        moment_ref,
        sum_ref,
        slope_ref,
    )
    sums = sum_ref[0:30, :] + sum_ref[30:60, :] + sum_ref[60:90, :]
    vortex = rows_of(src_ref[...], 3, 3)
    velocity, stretch = combine(points, vortex, sums)
    velocity_ref[...] = jnp.concatenate(velocity, axis=0)

    values = [inverse_volume * (a + time_step * d) for a, d in zip(vortex, stretch)]
    values.append(inverse_volume * dye_ref[...])
    cell = cell_ref[...]
    starts = [cell & 7, (cell >> 3) & 3, cell >> 5]
    bases, fractions = [], []
    for d in range(3):
        place = starts[d].astype(f32) + frac_ref[d : d + 1, :] + move_scale * velocity[d]
        lowest = jnp.floor(place)
        bases.append(lowest.astype(jnp.int32))
        fractions.append(place - lowest)
    node = lax.broadcasted_iota(jnp.int32, (8, count), 0)
    weight_x = axis_weights(node, bases[0], fractions[0], 8)
    node = lax.broadcasted_iota(jnp.int32, (16, count), 0)
    weight_zy = axis_weights(node & 3, bases[1], fractions[1], 4) * axis_weights(
        node >> 2, bases[2], fractions[2], 4
    )
    spread = jnp.concatenate([weight_zy[k : k + 1] * weight_x for k in range(16)], axis=0)
    spread_high = spread.astype(bf16)
    spread_low = (spread - spread_high.astype(f32)).astype(bf16)
    spread_both = jnp.concatenate([spread_high, spread_low], axis=0)

    slot = owner_ref[...] ^ lax.axis_index("dom")
    slot = (slot & 1) * (owners // 2) + (slot >> 1)
    node = lax.broadcasted_iota(jnp.int32, (16, count), 0)
    mine = slot * tiles + tile_ref[...] - (node >> 2)
    value = jnp.concatenate(values * 4, axis=0)
    value_high = value.astype(bf16).astype(f32)
    value_low = value - value_high
    total = owners * tiles * 4
    for group in range(total // 16):
        mask = mine == 4 * group
        first = 16 * group
        pick_ref[first : first + 16, :] = jnp.where(mask, value_high, 0.0).astype(bf16)
        first = total + 16 * group
        pick_ref[first : first + 16, :] = jnp.where(mask, value_low, 0.0).astype(bf16)
    both = lax.dot_general(
        pick_ref[...], spread_both, transposed_rhs, preferred_element_type=f32
    )
    both = both[:, 0:128] + both[:, 128:256]
    both = both[:total] + both[total:]
    keep_ref[...] = both[: total // 2]
    send_ref[...] = both[total // 2 :]


def vmem_specs(count):
    return [pl.BlockSpec(memory_space=pltpu.VMEM)] * count


def on_device(
    positions, strength, core_radius, dye_amount, cell_fraction, cell_index, tile_local, owner_dom
):
    count = positions.shape[1]
    tiles = count // 128
    owners = lax.axis_size("dom")
    blocks = lax.axis_size("blk")
    width = math.gcd(count, 256)
    sources = jnp.concatenate([positions, strength, core_radius[None]], axis=0)
    others = [
        lax.ppermute(sources, "blk", [(i, (i + s) % blocks) for i in range(blocks)])
        for s in range(1, blocks)
    ]
    scratch = lambda n: [
        pltpu.VMEM((48, count), bf16),
        pltpu.VMEM((n * count, 48), bf16),
        pltpu.VMEM((96, n * count), bf16),
        pltpu.VMEM((min(8, count // width), 2 * width, width), bf16),
    ]
    params = pltpu.CompilerParams(vmem_limit_bytes=48 * 2**20)
    cost = lambda n: pl.CostEstimate(
        flops=n * count * count * 256 * 2 * 3,
        bytes_accessed=4 * count * 256,
        transcendentals=n * count * count,
    )
    own_sums = pl.pallas_call(
        own_kernel,
        out_shape=jax.ShapeDtypeStruct((96, count), f32),
        in_specs=vmem_specs(2),
        out_specs=vmem_specs(1)[0],
        scratch_shapes=scratch(1),
        compiler_params=params,
        cost_estimate=cost(1),
        name="own_pairs",
    )(positions, sources)
    half = jax.ShapeDtypeStruct((owners * tiles * 2, 128), f32)
    velocity, keep, send = pl.pallas_call(
        functools.partial(tail_kernel, tiles, owners),
        out_shape=(jax.ShapeDtypeStruct((3, count), f32), half, half),
        in_specs=vmem_specs(8 + len(others)),
        out_specs=tuple(vmem_specs(3)),
        scratch_shapes=scratch(len(others))
        + [pltpu.VMEM((96, count), f32), pltpu.VMEM((owners * tiles * 8, count), bf16)],
        compiler_params=params,
        cost_estimate=cost(len(others)),
        name="other_pairs_and_deposit",
    )(
        positions,
        sources,
        own_sums,
        dye_amount[None],
        cell_fraction,
        cell_index[None],
        tile_local[None],
        owner_dom.reshape(1, count),
        *others,
    )
    exchange = lambda x, s: lax.ppermute(x, "dom", [(i, i ^ s) for i in range(owners)])
    grid = (keep + exchange(send, 1)).reshape(owners // 2, tiles, 4, 128)
    got = [exchange(grid[j], 2 * j) for j in range(owners // 2 - 1, 0, -1)]
    return velocity, sum(got, grid[0])


def solution(mesh):
    both = ("dom", "blk")
    placed = (
        P(None, both),
        P(None, both),
        P(both),
        P(both),
        P(None, both),
        P(both),
        P(both),
        P(both, None),
    )
    return jax.shard_map(
        on_device,
        mesh=mesh,
        in_specs=placed,
        out_specs=(P(None, both), P(both, None, None)),
        check_vma=False,
    )
```

```python
import functools
import math

import jax
import jax.numpy as jnp
from jax import lax
from jax.experimental import pallas as pl
from jax.experimental.pallas import tpu as pltpu
from jax.sharding import PartitionSpec as P

time_step = 0.02
move_scale = 2.0
inverse_volume = 32.0
kernel_scale = 1.0 / (4.0 * math.pi)
f32 = jnp.float32
bf16 = jnp.bfloat16
transposed_rhs = (((1,), (1,)), ((), ()))


def split3(x):
    high = x.astype(bf16).astype(f32)
    rest = x - high
    middle = rest.astype(bf16).astype(f32)
    return high, middle, rest - middle


def rows_of(array, first, count):
    return [array[first + d : first + d + 1] for d in range(count)]


def cross_rows(left, right):
    return [
        left[1] * right[2] - left[2] * right[1],
        left[2] * right[0] - left[0] * right[2],
        left[0] * right[1] - left[1] * right[0],
    ]


def square_sum(rows):
    return rows[0] * rows[0] + rows[1] * rows[1] + rows[2] * rows[2]


def target_features(points):
    one = jnp.ones_like(points[0])
    zero = jnp.zeros_like(one)
    stack = jnp.concatenate(points + [one, square_sum(points), zero, zero, zero], axis=0)
    high, middle, low = split3(stack)
    return jnp.concatenate([high, middle, high, low, high, middle], axis=0)


def source_features(src):
    points = rows_of(src, 0, 3)
    vortex = rows_of(src, 3, 3)
    radius = src[6:7]
    offset = square_sum(points) + radius * radius
    one = jnp.ones_like(radius)
    zero = jnp.zeros_like(radius)
    stack = jnp.concatenate([-2.0 * p for p in points] + [offset, one, zero, zero, zero], axis=0)
    high, middle, low = split3(stack)
    features = jnp.concatenate([high, high, middle, high, low, middle], axis=0)
    base = jnp.concatenate(vortex + cross_rows(vortex, points), axis=0)
    groups = jnp.concatenate([base] + [base * p for p in points] + [base * offset], axis=0)
    moments = jnp.concatenate(list(split3(groups)) + [jnp.zeros_like(base)], axis=0)
    return features.T.astype(bf16), moments.astype(bf16)


def add_pair_sums(lag, unroll, target_ref, feature_ref, moment_ref, sum_ref, slope_ref):
    targets = sum_ref.shape[1]
    slots, chunk, width = slope_ref.shape
    chunk = chunk // 2
    chunks = feature_ref.shape[0] // chunk
    tiles = targets // width
    lag = min(lag, chunks)

    def produce(start, number):
        square = jnp.dot(
            feature_ref[number * chunk : (number + 1) * chunk, :],
            target_ref[:, pl.ds(start, width)],
            preferred_element_type=f32,
        )
        inverse = lax.rsqrt(square)
        inverse2 = inverse * inverse
        slope = inverse2 * inverse2 * inverse
        high = slope.astype(bf16)
        slope_ref[number % slots, :chunk] = high
        slope_ref[number % slots, chunk:] = (slope - high.astype(f32)).astype(bf16)

    def consume(start, number):
        moments = moment_ref[:, number * chunk : (number + 1) * chunk]
        sum_ref[:, pl.ds(start, width)] += jnp.dot(
            moments, slope_ref[number % slots, :chunk], preferred_element_type=f32
        ) + jnp.dot(moments, slope_ref[number % slots, chunk:], preferred_element_type=f32)

    for number in range(chunks - lag, chunks):
        slope_ref[number % slots] = jnp.zeros(slope_ref.shape[1:], bf16)

    def step(k, carry):
        for u in range(unroll):
            start = pl.multiple_of((k * unroll + u) * width, width)
            before = pl.multiple_of(jnp.maximum(k * unroll + u - 1, 0) * width, width)
            for number in range(chunks):
                if number >= lag:
                    consume(start, number - lag)
                else:
                    consume(before, number - lag + chunks)
                produce(start, number)
        return carry

    lax.fori_loop(0, tiles // unroll, step, 0)
    for number in range(chunks - lag, chunks):
        consume((tiles - 1) * width, number)


def own_kernel(
    pos_ref, src_ref, sum_ref, target_ref, feature_ref, moment_ref, slope_ref
):
    target_ref[...] = target_features(rows_of(pos_ref[...], 0, 3)).astype(bf16)
    feature_ref[...], moment_ref[...] = source_features(src_ref[...])
    sum_ref[...] = jnp.zeros_like(sum_ref)
    tiles = sum_ref.shape[1] // slope_ref.shape[2]
    add_pair_sums(
        4, math.gcd(tiles, 8), target_ref, feature_ref, moment_ref, sum_ref, slope_ref
    )


def combine(points, vortex, sums):
    plain, by_x, by_y, by_z, by_offset = [sums[6 * k : 6 * k + 6] for k in range(5)]
    kernel = (
        square_sum(points) * plain
        + by_offset
        - 2.0 * (points[0] * by_x + points[1] * by_y + points[2] * by_z)
    ) * kernel_scale
    along = points[0] * vortex[0] + points[1] * vortex[1] + points[2] * vortex[2]
    slope = (along * plain - vortex[0] * by_x - vortex[1] * by_y - vortex[2] * by_z) * (
        -3.0 * kernel_scale
    )
    kernel_a = rows_of(kernel, 0, 3)
    velocity = [u - v for u, v in zip(cross_rows(kernel_a, points), rows_of(kernel, 3, 3))]
    term_one = cross_rows(kernel_a, vortex)
    slope_a = rows_of(slope, 0, 3)
    term_two = [u - v for u, v in zip(cross_rows(slope_a, points), rows_of(slope, 3, 3))]
    return velocity, [u + v for u, v in zip(term_one, term_two)]


def axis_weights(node, base, fraction, cells):
    t = fraction
    s = 1.0 - t
    inner = [1.0 - 2.5 * u * u + 1.5 * u * u * u for u in (t, s)]
    weights = [-0.5 * s * s * t, inner[0], inner[1], -0.5 * t * t * s]
    place = (node - base + 1) & (cells - 1)
    out = jnp.zeros(node.shape, f32)
    for k in range(4):
        out = jnp.where(place == k, weights[k], out)
    return out


def tail_kernel(
    tiles,
    owners,
    pos_ref,
    src_ref,
    before_ref,
    dye_ref,
    frac_ref,
    cell_ref,
    tile_ref,
    owner_ref,
    *refs,
):
    other_refs = refs[:-12]
    velocity_ref, value_ref, spread_ref, send_ref, *refs = refs[-12:]
    target_ref, feature_ref, moment_ref, slope_ref, sum_ref, pick_ref, ready_ref, copied = refs
    count = src_ref.shape[1]
    points = rows_of(pos_ref[...], 0, 3)
    target_ref[...] = target_features(points).astype(bf16)
    for k, other_ref in enumerate(other_refs):
        place = slice(k * count, (k + 1) * count)
        feature_ref[place], moment_ref[:, place] = source_features(other_ref[...])
    sum_ref[...] = before_ref[...]
    add_pair_sums(
        8,
        math.gcd(count // slope_ref.shape[2], 2),
        target_ref,
        feature_ref,
        moment_ref,
        sum_ref,
        slope_ref,
    )
    sums = sum_ref[0:30, :] + sum_ref[30:60, :] + sum_ref[60:90, :]
    vortex = rows_of(src_ref[...], 3, 3)
    velocity, stretch = combine(points, vortex, sums)
    ready_ref[...] = jnp.concatenate(velocity, axis=0)
    velocity_copy = pltpu.make_async_copy(ready_ref, velocity_ref, copied)
    velocity_copy.start()

    values = [inverse_volume * (a + time_step * d) for a, d in zip(vortex, stretch)]
    values.append(inverse_volume * dye_ref[...])
    cell = cell_ref[...]
    starts = [cell & 7, (cell >> 3) & 3, cell >> 5]
    bases, fractions = [], []
    for d in range(3):
        place = starts[d].astype(f32) + frac_ref[d : d + 1, :] + move_scale * velocity[d]
        lowest = jnp.floor(place)
        bases.append(lowest.astype(jnp.int32))
        fractions.append(place - lowest)
    node = lax.broadcasted_iota(jnp.int32, (8, count), 0)
    weight_x = axis_weights(node, bases[0], fractions[0], 8)
    node = lax.broadcasted_iota(jnp.int32, (16, count), 0)
    weight_zy = axis_weights(node & 3, bases[1], fractions[1], 4) * axis_weights(
        node >> 2, bases[2], fractions[2], 4
    )
    spread = jnp.concatenate([weight_zy[k : k + 1] * weight_x for k in range(16)], axis=0)
    spread_high = spread.astype(bf16)
    spread_low = (spread - spread_high.astype(f32)).astype(bf16)
    spread_both = jnp.concatenate([spread_high, spread_low], axis=0)

    value_ref[...] = jnp.concatenate(values, axis=0)
    spread_ref[...] = spread_both
    send_ref[...] = deposits(
        tiles, owners, 1, owner_ref[...], tile_ref[...], value_ref[...], spread_both, pick_ref
    )
    velocity_copy.wait()


def deposits(tiles, owners, odd, owner, tile, value, spread_both, pick_ref):
    count = owner.shape[1]
    slot = owner ^ lax.axis_index("dom")
    number = jnp.where((slot & 1) == odd, (slot >> 1) * tiles + tile, -8)
    node = lax.broadcasted_iota(jnp.int32, (16, count), 0)
    mine = number - (node >> 2)
    value = jnp.concatenate([value] * 4, axis=0)
    value_high = value.astype(bf16).astype(f32)
    value_low = value - value_high
    total = owners * tiles * 2
    for group in range(total // 16):
        mask = mine == 4 * group
        first = 16 * group
        pick_ref[first : first + 16, :] = jnp.where(mask, value_high, 0.0).astype(bf16)
        first = total + 16 * group
        pick_ref[first : first + 16, :] = jnp.where(mask, value_low, 0.0).astype(bf16)
    both = lax.dot_general(
        pick_ref[...], spread_both, transposed_rhs, preferred_element_type=f32
    )
    both = both[:, 0:128] + both[:, 128:256]
    return both[:total] + both[total:]


def keep_kernel(tiles, owners, value_ref, spread_ref, tile_ref, owner_ref, keep_ref, pick_ref):
    keep_ref[...] = deposits(
        tiles, owners, 0, owner_ref[...], tile_ref[...], value_ref[...], spread_ref[...], pick_ref
    )


def vmem_specs(count):
    return [pl.BlockSpec(memory_space=pltpu.VMEM)] * count


def partner(i, step, count):
    return i ^ step if count & (count - 1) == 0 else (i + step) % count


def on_device(
    positions, strength, core_radius, dye_amount, cell_fraction, cell_index, tile_local, owner_dom
):
    count = positions.shape[1]
    tiles = count // 128
    owners = lax.axis_size("dom")
    blocks = lax.axis_size("blk")
    width = math.gcd(count, 256)
    sources = jnp.concatenate([positions, strength, core_radius[None]], axis=0)
    others = [
        lax.ppermute(sources, "blk", [(i, partner(i, s, blocks)) for i in range(blocks)])
        for s in range(1, blocks)
    ]
    scratch = lambda n: [
        pltpu.VMEM((48, count), bf16),
        pltpu.VMEM((n * count, 48), bf16),
        pltpu.VMEM((96, n * count), bf16),
        pltpu.VMEM((min(8, count // width), 2 * width, width), bf16),
    ]
    params = pltpu.CompilerParams(vmem_limit_bytes=48 * 2**20)
    cost = lambda n: pl.CostEstimate(
        flops=n * count * count * 256 * 2 * 3,
        bytes_accessed=4 * count * 256,
        transcendentals=n * count * count,
    )
    own_sums = pl.pallas_call(
        own_kernel,
        out_shape=jax.ShapeDtypeStruct((96, count), f32),
        in_specs=vmem_specs(2),
        out_specs=vmem_specs(1)[0],
        scratch_shapes=scratch(1),
        compiler_params=params,
        cost_estimate=cost(1),
        name="own_pairs",
    )(positions, sources)
    half = jax.ShapeDtypeStruct((owners * tiles * 2, 128), f32)
    pick = pltpu.VMEM((owners * tiles * 4, count), bf16)
    tile_row = tile_local[None]
    owner_row = owner_dom.reshape(1, count)
    velocity, value, spread, send = pl.pallas_call(
        functools.partial(tail_kernel, tiles, owners),
        out_shape=(
            jax.ShapeDtypeStruct((3, count), f32),
            jax.ShapeDtypeStruct((4, count), f32),
            jax.ShapeDtypeStruct((256, count), bf16),
            half,
        ),
        in_specs=vmem_specs(8 + len(others)),
        out_specs=(pl.BlockSpec(memory_space=pl.ANY), *vmem_specs(3)),
        scratch_shapes=scratch(len(others))
        + [
            pltpu.VMEM((96, count), f32),
            pick,
            pltpu.VMEM((3, count), f32),
            pltpu.SemaphoreType.DMA,
        ],
        compiler_params=params,
        cost_estimate=cost(len(others)),
        name="other_pairs_and_deposit",
    )(
        positions,
        sources,
        own_sums,
        dye_amount[None],
        cell_fraction,
        cell_index[None],
        tile_row,
        owner_row,
        *others,
    )
    keep = pl.pallas_call(
        functools.partial(keep_kernel, tiles, owners),
        out_shape=half,
        in_specs=vmem_specs(4),
        out_specs=vmem_specs(1)[0],
        scratch_shapes=[pick],
        compiler_params=params,
        cost_estimate=pl.CostEstimate(
            flops=owners * tiles * 8 * count * 256 * 2,
            bytes_accessed=count * 1024,
            transcendentals=0,
        ),
        name="deposit_even_slots",
    )(value, spread, tile_row, owner_row)
    exchange = lambda x, s: lax.ppermute(x, "dom", [(i, i ^ s) for i in range(owners)])
    grid = (keep + exchange(send, 1)).reshape(owners // 2, tiles, 4, 128)
    got = [exchange(grid[j], 2 * j) for j in range(owners // 2 - 1, 0, -1)]
    return velocity, sum(got, grid[0])


def solution(mesh):
    both = ("dom", "blk")
    placed = (
        P(None, both),
        P(None, both),
        P(both),
        P(both),
        P(None, both),
        P(both),
        P(both),
        P(both, None),
    )
    return jax.shard_map(
        on_device,
        mesh=mesh,
        in_specs=placed,
        out_specs=(P(None, both), P(both, None, None)),
        check_vma=False,
    )
```

```python
import functools
import math

import jax
import jax.numpy as jnp
from jax import lax
from jax.experimental import pallas as pl
from jax.experimental.pallas import tpu as pltpu
from jax.sharding import PartitionSpec as P

time_step = 0.02
move_scale = 2.0
inverse_volume = 32.0
kernel_scale = 1.0 / (4.0 * math.pi)
f32 = jnp.float32
bf16 = jnp.bfloat16
transposed_rhs = (((1,), (1,)), ((), ()))


def split3(x):
    high = x.astype(bf16)
    rest = x - high.astype(f32)
    middle = rest.astype(bf16)
    return high, middle, (rest - middle.astype(f32)).astype(bf16)


def rows_of(array, first, count):
    return [array[first + d : first + d + 1] for d in range(count)]


def cross_rows(left, right):
    return [
        left[1] * right[2] - left[2] * right[1],
        left[2] * right[0] - left[0] * right[2],
        left[0] * right[1] - left[1] * right[0],
    ]


def square_sum(rows):
    return rows[0] * rows[0] + rows[1] * rows[1] + rows[2] * rows[2]


def target_features(points):
    one = jnp.ones_like(points[0])
    zero = jnp.zeros_like(one)
    stack = jnp.concatenate(points + [one, square_sum(points), zero, zero, zero], axis=0)
    high, middle, low = [part.astype(f32) for part in split3(stack)]
    return jnp.concatenate([high, middle, high, low, high, middle], axis=0).astype(bf16)


def source_features(src):
    points = rows_of(src, 0, 3)
    vortex = rows_of(src, 3, 3)
    radius = src[6:7]
    offset = square_sum(points) + radius * radius
    one = jnp.ones_like(radius)
    zero = jnp.zeros_like(radius)
    stack = jnp.concatenate([-2.0 * p for p in points] + [offset, one, zero, zero, zero], axis=0)
    high, middle, low = [part.astype(f32) for part in split3(stack)]
    features = jnp.concatenate([high, high, middle, high, low, middle], axis=0)
    base = jnp.concatenate(vortex + cross_rows(vortex, points), axis=0)
    groups = jnp.concatenate(
        [base] + [base * p for p in points] + [base * offset, zero, zero], axis=0
    )
    return features.T.astype(bf16), jnp.concatenate(split3(groups), axis=0)


def add_pair_sums(lag, unroll, target_ref, feature_ref, moment_ref, sum_ref, slope_ref):
    targets = sum_ref.shape[1]
    slots, chunk, width = slope_ref.shape
    chunk = chunk // 2
    chunks = feature_ref.shape[0] // chunk
    tiles = targets // width
    lag = min(lag, chunks)

    def produce(start, number):
        square = jnp.dot(
            feature_ref[number * chunk : (number + 1) * chunk, :],
            target_ref[:, pl.ds(start, width)],
            preferred_element_type=f32,
        )
        inverse = lax.rsqrt(square)
        inverse2 = inverse * inverse
        slope = inverse2 * inverse2 * inverse
        high = slope.astype(bf16)
        slope_ref[number % slots, :chunk] = high
        slope_ref[number % slots, chunk:] = (slope - high.astype(f32)).astype(bf16)

    def consume(start, number):
        moments = moment_ref[:, number * chunk : (number + 1) * chunk]
        sum_ref[:, pl.ds(start, width)] += jnp.dot(
            moments, slope_ref[number % slots, :chunk], preferred_element_type=f32
        ) + jnp.dot(moments, slope_ref[number % slots, chunk:], preferred_element_type=f32)

    for number in range(chunks - lag, chunks):
        slope_ref[number % slots] = jnp.zeros(slope_ref.shape[1:], bf16)

    def step(k, carry):
        for u in range(unroll):
            start = pl.multiple_of((k * unroll + u) * width, width)
            before = pl.multiple_of(jnp.maximum(k * unroll + u - 1, 0) * width, width)
            for number in range(chunks):
                if number >= lag:
                    consume(start, number - lag)
                else:
                    consume(before, number - lag + chunks)
                produce(start, number)
        return carry

    lax.fori_loop(0, tiles // unroll, step, 0)
    for number in range(chunks - lag, chunks):
        consume((tiles - 1) * width, number)


def own_kernel(
    pos_ref, src_ref, sum_ref, target_ref, feature_ref, moment_ref, slope_ref
):
    target_ref[...] = target_features(rows_of(pos_ref[...], 0, 3))
    feature_ref[...], moment_ref[...] = source_features(src_ref[...])
    sum_ref[...] = jnp.zeros_like(sum_ref)
    tiles = sum_ref.shape[1] // slope_ref.shape[2]
    add_pair_sums(
        4, math.gcd(tiles, 8), target_ref, feature_ref, moment_ref, sum_ref, slope_ref
    )


def combine(points, vortex, sums):
    plain, by_x, by_y, by_z, by_offset = [sums[6 * k : 6 * k + 6] for k in range(5)]
    kernel = (
        square_sum(points) * plain
        + by_offset
        - 2.0 * (points[0] * by_x + points[1] * by_y + points[2] * by_z)
    ) * kernel_scale
    along = points[0] * vortex[0] + points[1] * vortex[1] + points[2] * vortex[2]
    slope = (along * plain - vortex[0] * by_x - vortex[1] * by_y - vortex[2] * by_z) * (
        -3.0 * kernel_scale
    )
    kernel_a = rows_of(kernel, 0, 3)
    velocity = [u - v for u, v in zip(cross_rows(kernel_a, points), rows_of(kernel, 3, 3))]
    term_one = cross_rows(kernel_a, vortex)
    slope_a = rows_of(slope, 0, 3)
    term_two = [u - v for u, v in zip(cross_rows(slope_a, points), rows_of(slope, 3, 3))]
    return velocity, [u + v for u, v in zip(term_one, term_two)]


def axis_weights(node, base, fraction, cells):
    t = fraction
    s = 1.0 - t
    inner = [1.0 - 2.5 * u * u + 1.5 * u * u * u for u in (t, s)]
    weights = [-0.5 * s * s * t, inner[0], inner[1], -0.5 * t * t * s]
    place = (node - base + 1) & (cells - 1)
    out = jnp.zeros(node.shape, f32)
    for k in range(4):
        out = jnp.where(place == k, weights[k], out)
    return out


def tail_kernel(
    tiles,
    owners,
    pos_ref,
    src_ref,
    before_ref,
    dye_ref,
    frac_ref,
    cell_ref,
    tile_ref,
    owner_ref,
    *refs,
):
    other_refs = refs[:-12]
    velocity_ref, value_ref, spread_ref, send_ref, *refs = refs[-12:]
    target_ref, feature_ref, moment_ref, slope_ref, sum_ref, pick_ref, ready_ref, copied = refs
    count = src_ref.shape[1]
    points = rows_of(pos_ref[...], 0, 3)
    target_ref[...] = target_features(points)
    for k, other_ref in enumerate(other_refs):
        place = slice(k * count, (k + 1) * count)
        feature_ref[place], moment_ref[:, place] = source_features(other_ref[...])
    sum_ref[...] = before_ref[...]
    add_pair_sums(
        8,
        math.gcd(count // slope_ref.shape[2], 2),
        target_ref,
        feature_ref,
        moment_ref,
        sum_ref,
        slope_ref,
    )
    sums = sum_ref[0:32, :] + sum_ref[32:64, :] + sum_ref[64:96, :]
    vortex = rows_of(src_ref[...], 3, 3)
    velocity, stretch = combine(points, vortex, sums)
    ready_ref[...] = jnp.concatenate(velocity, axis=0)
    velocity_copy = pltpu.make_async_copy(ready_ref, velocity_ref, copied)
    velocity_copy.start()

    values = [inverse_volume * (a + time_step * d) for a, d in zip(vortex, stretch)]
    values.append(inverse_volume * dye_ref[...])
    cell = cell_ref[...]
    starts = [cell & 7, (cell >> 3) & 3, cell >> 5]
    bases, fractions = [], []
    for d in range(3):
        place = starts[d].astype(f32) + frac_ref[d : d + 1, :] + move_scale * velocity[d]
        lowest = jnp.floor(place)
        bases.append(lowest.astype(jnp.int32))
        fractions.append(place - lowest)
    node = lax.broadcasted_iota(jnp.int32, (8, count), 0)
    weight_x = axis_weights(node, bases[0], fractions[0], 8)
    node = lax.broadcasted_iota(jnp.int32, (16, count), 0)
    weight_zy = axis_weights(node & 3, bases[1], fractions[1], 4) * axis_weights(
        node >> 2, bases[2], fractions[2], 4
    )
    spread = jnp.concatenate([weight_zy[k : k + 1] * weight_x for k in range(16)], axis=0)
    spread_high = spread.astype(bf16)
    spread_low = (spread - spread_high.astype(f32)).astype(bf16)
    spread_both = jnp.concatenate([spread_high, spread_low], axis=0)

    value_ref[...] = jnp.concatenate(values, axis=0)
    spread_ref[...] = spread_both
    send_ref[...] = deposits(
        tiles, owners, 1, owner_ref[...], tile_ref[...], value_ref[...], spread_both, pick_ref
    )
    velocity_copy.wait()


def slots_of(owners):
    if owners == 8:
        return (0, 6, 2, 3), (1, 7, 5, 4)
    return range(0, owners, 2), range(1, owners, 2)


def deposits(tiles, owners, odd, owner, tile, value, spread_both, pick_ref):
    count = owner.shape[1]
    me = lax.axis_index("dom")
    slot = owner ^ me
    if owners == 8:
        traded = (slot & 1) | ((slot & 2) << 1) | ((slot & 4) >> 1)
        slot = jnp.where((me & 1) == 1, traded, slot)
    number = jnp.full(slot.shape, -8, jnp.int32)
    for place, s in enumerate(slots_of(owners)[odd]):
        number = jnp.where(slot == s, place * tiles + tile, number)
    node = lax.broadcasted_iota(jnp.int32, (16, count), 0)
    mine = number - (node >> 2)
    value = jnp.concatenate([value] * 4, axis=0)
    value_high = value.astype(bf16).astype(f32)
    value_low = value - value_high
    total = owners * tiles * 2
    for group in range(total // 16):
        mask = mine == 4 * group
        first = 16 * group
        pick_ref[first : first + 16, :] = jnp.where(mask, value_high, 0.0).astype(bf16)
        first = total + 16 * group
        pick_ref[first : first + 16, :] = jnp.where(mask, value_low, 0.0).astype(bf16)
    both = lax.dot_general(
        pick_ref[...], spread_both, transposed_rhs, preferred_element_type=f32
    )
    both = both[:, 0:128] + both[:, 128:256]
    return both[:total] + both[total:]


def keep_kernel(tiles, owners, value_ref, spread_ref, tile_ref, owner_ref, keep_ref, pick_ref):
    keep_ref[...] = deposits(
        tiles, owners, 0, owner_ref[...], tile_ref[...], value_ref[...], spread_ref[...], pick_ref
    )


def vmem_specs(count):
    return [pl.BlockSpec(memory_space=pltpu.VMEM)] * count


def partner(i, step, count):
    return i ^ step if count & (count - 1) == 0 else (i + step) % count


def on_device(
    positions, strength, core_radius, dye_amount, cell_fraction, cell_index, tile_local, owner_dom
):
    count = positions.shape[1]
    tiles = count // 128
    owners = lax.axis_size("dom")
    blocks = lax.axis_size("blk")
    width = math.gcd(count, 256)
    sources = jnp.concatenate([positions, strength, core_radius[None]], axis=0)
    others = [
        lax.ppermute(sources, "blk", [(i, partner(i, s, blocks)) for i in range(blocks)])
        for s in range(1, blocks)
    ]
    scratch = lambda n: [
        pltpu.VMEM((48, count), bf16),
        pltpu.VMEM((n * count, 48), bf16),
        pltpu.VMEM((96, n * count), bf16),
        pltpu.VMEM((min(8, count // width), 2 * width, width), bf16),
    ]
    params = pltpu.CompilerParams(vmem_limit_bytes=48 * 2**20)
    cost = lambda n: pl.CostEstimate(
        flops=n * count * count * 256 * 2 * 3,
        bytes_accessed=4 * count * 256,
        transcendentals=n * count * count,
    )
    own_sums = pl.pallas_call(
        own_kernel,
        out_shape=jax.ShapeDtypeStruct((96, count), f32),
        in_specs=vmem_specs(2),
        out_specs=vmem_specs(1)[0],
        scratch_shapes=scratch(1),
        compiler_params=params,
        cost_estimate=cost(1),
        name="own_pairs",
    )(positions, sources)
    half = jax.ShapeDtypeStruct((owners * tiles * 2, 128), f32)
    pick = pltpu.VMEM((owners * tiles * 4, count), bf16)
    tile_row = tile_local[None]
    owner_row = owner_dom.reshape(1, count)
    velocity, value, spread, send = pl.pallas_call(
        functools.partial(tail_kernel, tiles, owners),
        out_shape=(
            jax.ShapeDtypeStruct((3, count), f32),
            jax.ShapeDtypeStruct((4, count), f32),
            jax.ShapeDtypeStruct((256, count), bf16),
            half,
        ),
        in_specs=vmem_specs(8 + len(others)),
        out_specs=(pl.BlockSpec(memory_space=pl.ANY), *vmem_specs(3)),
        scratch_shapes=scratch(len(others))
        + [
            pltpu.VMEM((96, count), f32),
            pick,
            pltpu.VMEM((3, count), f32),
            pltpu.SemaphoreType.DMA,
        ],
        compiler_params=params,
        cost_estimate=cost(len(others)),
        name="other_pairs_and_deposit",
    )(
        positions,
        sources,
        own_sums,
        dye_amount[None],
        cell_fraction,
        cell_index[None],
        tile_row,
        owner_row,
        *others,
    )
    keep = pl.pallas_call(
        functools.partial(keep_kernel, tiles, owners),
        out_shape=half,
        in_specs=vmem_specs(4),
        out_specs=vmem_specs(1)[0],
        scratch_shapes=[pick],
        compiler_params=params,
        cost_estimate=pl.CostEstimate(
            flops=owners * tiles * 8 * count * 256 * 2,
            bytes_accessed=count * 1024,
            transcendentals=0,
        ),
        name="deposit_even_slots",
    )(value, spread, tile_row, owner_row)
    exchange = lambda x, s: lax.ppermute(x, "dom", [(i, i ^ s) for i in range(owners)])
    grid = (keep + exchange(send, 1)).reshape(owners // 2, tiles, 4, 128)
    if owners == 8:
        near = lax.ppermute(grid[2:], "dom", [(i, i ^ (4 if i & 1 else 2)) for i in range(owners)])
        far = exchange(grid[1], 6)
        return velocity, grid[0] + near[0] + far + exchange(near[1], 1)
    got = [exchange(grid[j], 2 * j) for j in range(owners // 2 - 1, 0, -1)]
    return velocity, sum(got, grid[0])


def solution(mesh):
    both = ("dom", "blk")
    placed = (
        P(None, both),
        P(None, both),
        P(both),
        P(both),
        P(None, both),
        P(both),
        P(both),
        P(both, None),
    )
    return jax.shard_map(
        on_device,
        mesh=mesh,
        in_specs=placed,
        out_specs=(P(None, both), P(both, None, None)),
        check_vma=False,
    )
```

```python
import functools
import math

import jax
import jax.numpy as jnp
from jax import lax
from jax.experimental import pallas as pl
from jax.experimental.pallas import tpu as pltpu
from jax.sharding import PartitionSpec as P

time_step = 0.02
move_scale = 2.0
inverse_volume = 32.0
kernel_scale = 1.0 / (4.0 * math.pi)
f32 = jnp.float32
bf16 = jnp.bfloat16
transposed_rhs = (((1,), (1,)), ((), ()))


def split3(x):
    high = x.astype(bf16)
    rest = x - high.astype(f32)
    middle = rest.astype(bf16)
    return high, middle, (rest - middle.astype(f32)).astype(bf16)


def rows_of(array, first, count):
    return [array[first + d : first + d + 1] for d in range(count)]


def cross_rows(left, right):
    return [
        left[1] * right[2] - left[2] * right[1],
        left[2] * right[0] - left[0] * right[2],
        left[0] * right[1] - left[1] * right[0],
    ]


def square_sum(rows):
    return rows[0] * rows[0] + rows[1] * rows[1] + rows[2] * rows[2]


def target_features(points):
    one = jnp.ones_like(points[0])
    zero = jnp.zeros_like(one)
    stack = jnp.concatenate(points + [one, square_sum(points), zero, zero, zero], axis=0)
    high, middle, low = [part.astype(f32) for part in split3(stack)]
    return jnp.concatenate([high, middle, high, low, high, middle], axis=0).astype(bf16)


def source_features(src):
    points = rows_of(src, 0, 3)
    vortex = rows_of(src, 3, 3)
    radius = src[6:7]
    offset = square_sum(points) + radius * radius
    one = jnp.ones_like(radius)
    zero = jnp.zeros_like(radius)
    stack = jnp.concatenate([-2.0 * p for p in points] + [offset, one, zero, zero, zero], axis=0)
    high, middle, low = [part.astype(f32) for part in split3(stack)]
    features = jnp.concatenate([high, high, middle, high, low, middle], axis=0)
    base = jnp.concatenate(vortex + cross_rows(vortex, points), axis=0)
    groups = jnp.concatenate(
        [base] + [base * p for p in points] + [base * offset, zero, zero], axis=0
    )
    return features.T.astype(bf16), jnp.concatenate(split3(groups), axis=0)


def add_pair_sums(lag, unroll, target_ref, feature_ref, moment_ref, sum_ref, slope_ref):
    targets = sum_ref.shape[1]
    slots, chunk, width = slope_ref.shape
    chunk = chunk // 2
    chunks = feature_ref.shape[0] // chunk
    tiles = targets // width
    lag = min(lag, chunks)

    def produce(start, number):
        square = jnp.dot(
            feature_ref[number * chunk : (number + 1) * chunk, :],
            target_ref[:, pl.ds(start, width)],
            preferred_element_type=f32,
        )
        inverse = lax.rsqrt(square)
        inverse2 = inverse * inverse
        slope = inverse2 * inverse2 * inverse
        high = slope.astype(bf16)
        slope_ref[number % slots, :chunk] = high
        slope_ref[number % slots, chunk:] = (slope - high.astype(f32)).astype(bf16)

    def consume(start, number):
        moments = moment_ref[:, number * chunk : (number + 1) * chunk]
        sum_ref[:, pl.ds(start, width)] += jnp.dot(
            moments, slope_ref[number % slots, :chunk], preferred_element_type=f32
        ) + jnp.dot(moments, slope_ref[number % slots, chunk:], preferred_element_type=f32)

    if tiles > unroll:
        for number in range(chunks - lag, chunks):
            slope_ref[number % slots] = jnp.zeros(slope_ref.shape[1:], bf16)

    def step(k, carry):
        for u in range(unroll):
            start = pl.multiple_of((k * unroll + u) * width, width)
            before = pl.multiple_of(jnp.maximum(k * unroll + u - 1, 0) * width, width)
            for number in range(chunks):
                if number >= lag:
                    consume(start, number - lag)
                elif u > 0 or tiles > unroll:
                    consume(before, number - lag + chunks)
                produce(start, number)
        return carry

    if tiles > unroll:
        lax.fori_loop(0, tiles // unroll, step, 0)
    else:
        step(0, 0)
    for number in range(chunks - lag, chunks):
        consume((tiles - 1) * width, number)


def own_kernel(
    pos_ref, src_ref, sum_ref, target_ref, feature_ref, moment_ref, slope_ref
):
    target_ref[...] = target_features(rows_of(pos_ref[...], 0, 3))
    feature_ref[...], moment_ref[...] = source_features(src_ref[...])
    sum_ref[...] = jnp.zeros_like(sum_ref)
    tiles = sum_ref.shape[1] // slope_ref.shape[2]
    add_pair_sums(
        8, math.gcd(tiles, 8), target_ref, feature_ref, moment_ref, sum_ref, slope_ref
    )


def combine(points, vortex, sums):
    plain, by_x, by_y, by_z, by_offset = [sums[6 * k : 6 * k + 6] for k in range(5)]
    kernel = (
        square_sum(points) * plain
        + by_offset
        - 2.0 * (points[0] * by_x + points[1] * by_y + points[2] * by_z)
    ) * kernel_scale
    along = points[0] * vortex[0] + points[1] * vortex[1] + points[2] * vortex[2]
    slope = (along * plain - vortex[0] * by_x - vortex[1] * by_y - vortex[2] * by_z) * (
        -3.0 * kernel_scale
    )
    kernel_a = rows_of(kernel, 0, 3)
    velocity = [u - v for u, v in zip(cross_rows(kernel_a, points), rows_of(kernel, 3, 3))]
    term_one = cross_rows(kernel_a, vortex)
    slope_a = rows_of(slope, 0, 3)
    term_two = [u - v for u, v in zip(cross_rows(slope_a, points), rows_of(slope, 3, 3))]
    return velocity, [u + v for u, v in zip(term_one, term_two)]


def axis_weights(node, base, fraction, cells):
    t = fraction
    s = 1.0 - t
    inner = [1.0 - 2.5 * u * u + 1.5 * u * u * u for u in (t, s)]
    weights = [-0.5 * s * s * t, inner[0], inner[1], -0.5 * t * t * s]
    place = (node - base + 1) & (cells - 1)
    out = jnp.zeros(node.shape, f32)
    for k in range(4):
        out = jnp.where(place == k, weights[k], out)
    return out


def tail_kernel(
    tiles,
    owners,
    pos_ref,
    src_ref,
    before_ref,
    dye_ref,
    frac_ref,
    cell_ref,
    tile_ref,
    owner_ref,
    *refs,
):
    other_refs = refs[:-12]
    velocity_ref, value_ref, spread_ref, send_ref, *refs = refs[-12:]
    target_ref, feature_ref, moment_ref, slope_ref, sum_ref, pick_ref, ready_ref, copied = refs
    count = src_ref.shape[1]
    points = rows_of(pos_ref[...], 0, 3)
    target_ref[...] = target_features(points)
    for k, other_ref in enumerate(other_refs):
        place = slice(k * count, (k + 1) * count)
        feature_ref[place], moment_ref[:, place] = source_features(other_ref[...])
    sum_ref[...] = before_ref[...]
    add_pair_sums(
        8,
        math.gcd(count // slope_ref.shape[2], 2),
        target_ref,
        feature_ref,
        moment_ref,
        sum_ref,
        slope_ref,
    )
    sums = sum_ref[0:32, :] + sum_ref[32:64, :] + sum_ref[64:96, :]
    vortex = rows_of(src_ref[...], 3, 3)
    velocity, stretch = combine(points, vortex, sums)
    ready_ref[...] = jnp.concatenate(velocity, axis=0)
    velocity_copy = pltpu.make_async_copy(ready_ref, velocity_ref, copied)
    velocity_copy.start()

    values = [inverse_volume * (a + time_step * d) for a, d in zip(vortex, stretch)]
    values.append(inverse_volume * dye_ref[...])
    cell = cell_ref[...]
    starts = [cell & 7, (cell >> 3) & 3, cell >> 5]
    bases, fractions = [], []
    for d in range(3):
        place = starts[d].astype(f32) + frac_ref[d : d + 1, :] + move_scale * velocity[d]
        lowest = jnp.floor(place)
        bases.append(lowest.astype(jnp.int32))
        fractions.append(place - lowest)
    node = lax.broadcasted_iota(jnp.int32, (8, count), 0)
    weight_x = axis_weights(node, bases[0], fractions[0], 8)
    node = lax.broadcasted_iota(jnp.int32, (16, count), 0)
    weight_zy = axis_weights(node & 3, bases[1], fractions[1], 4) * axis_weights(
        node >> 2, bases[2], fractions[2], 4
    )
    spread = jnp.concatenate([weight_zy[k : k + 1] * weight_x for k in range(16)], axis=0)
    spread_high = spread.astype(bf16)
    spread_low = (spread - spread_high.astype(f32)).astype(bf16)
    spread_both = jnp.concatenate([spread_high, spread_low], axis=0)

    value_ref[...] = jnp.concatenate(values, axis=0)
    spread_ref[...] = spread_both
    send_ref[...] = deposits(
        tiles,
        owners,
        slots_of(owners)[0],
        owner_ref[...],
        tile_ref[...],
        value_ref[...],
        spread_both,
        pick_ref,
    )
    velocity_copy.wait()


def slots_of(owners):
    if owners == 8:
        return (7, 5, 4), (6, 2, 3), (0, 1)
    return tuple(range(1, owners, 2)), tuple(range(0, owners, 2)), ()


def deposits(tiles, owners, slots, owner, tile, value, spread_both, pick_ref):
    count = owner.shape[1]
    me = lax.axis_index("dom")
    slot = owner ^ me
    if owners == 8:
        traded = (slot & 1) | ((slot & 2) << 1) | ((slot & 4) >> 1)
        slot = jnp.where((me & 1) == 1, traded, slot)
    number = jnp.full(slot.shape, -8, jnp.int32)
    for place, s in enumerate(slots):
        number = jnp.where(slot == s, place * tiles + tile, number)
    node = lax.broadcasted_iota(jnp.int32, (16, count), 0)
    mine = number - (node >> 2)
    value = jnp.concatenate([value] * 4, axis=0)
    value_high = value.astype(bf16).astype(f32)
    value_low = value - value_high
    total = len(slots) * tiles * 4
    for group in range(total // 16):
        mask = mine == 4 * group
        first = 16 * group
        pick_ref[first : first + 16, :] = jnp.where(mask, value_high, 0.0).astype(bf16)
        first = total + 16 * group
        pick_ref[first : first + 16, :] = jnp.where(mask, value_low, 0.0).astype(bf16)
    both = lax.dot_general(
        pick_ref[...], spread_both, transposed_rhs, preferred_element_type=f32
    )
    both = both[:, 0:128] + both[:, 128:256]
    return both[:total] + both[total:]


def deposit_kernel(
    tiles, owners, slots, value_ref, spread_ref, tile_ref, owner_ref, out_ref, pick_ref
):
    out_ref[...] = deposits(
        tiles,
        owners,
        slots,
        owner_ref[...],
        tile_ref[...],
        value_ref[...],
        spread_ref[...],
        pick_ref,
    )


def vmem_specs(count):
    return [pl.BlockSpec(memory_space=pltpu.VMEM)] * count


def partner(i, step, count):
    return i ^ step if count & (count - 1) == 0 else (i + step) % count


def on_device(
    positions, strength, core_radius, dye_amount, cell_fraction, cell_index, tile_local, owner_dom
):
    count = positions.shape[1]
    tiles = count // 128
    owners = lax.axis_size("dom")
    blocks = lax.axis_size("blk")
    width = math.gcd(count, 256)
    sources = jnp.concatenate([positions, strength, core_radius[None]], axis=0)
    others = [
        lax.ppermute(sources, "blk", [(i, partner(i, s, blocks)) for i in range(blocks)])
        for s in range(1, blocks)
    ]
    scratch = lambda n: [
        pltpu.VMEM((48, count), bf16),
        pltpu.VMEM((n * count, 48), bf16),
        pltpu.VMEM((96, n * count), bf16),
        pltpu.VMEM((min(8, count // width), 2 * width, width), bf16),
    ]
    params = pltpu.CompilerParams(vmem_limit_bytes=48 * 2**20)
    cost = lambda n: pl.CostEstimate(
        flops=n * count * count * 256 * 2 * 3,
        bytes_accessed=4 * count * 256,
        transcendentals=n * count * count,
    )
    own_sums = pl.pallas_call(
        own_kernel,
        out_shape=jax.ShapeDtypeStruct((96, count), f32),
        in_specs=vmem_specs(2),
        out_specs=vmem_specs(1)[0],
        scratch_shapes=scratch(1),
        compiler_params=params,
        cost_estimate=cost(1),
        name="own_pairs",
    )(positions, sources)
    sent, kept, apart = slots_of(owners)
    rows_for = lambda slots: jax.ShapeDtypeStruct((len(slots) * tiles * 4, 128), f32)
    pick_for = lambda slots: pltpu.VMEM((len(slots) * tiles * 8, count), bf16)
    tile_row = tile_local[None]
    owner_row = owner_dom.reshape(1, count)
    velocity, value, spread, send = pl.pallas_call(
        functools.partial(tail_kernel, tiles, owners),
        out_shape=(
            jax.ShapeDtypeStruct((3, count), f32),
            jax.ShapeDtypeStruct((4, count), f32),
            jax.ShapeDtypeStruct((256, count), bf16),
            rows_for(sent),
        ),
        in_specs=vmem_specs(8 + len(others)),
        out_specs=(pl.BlockSpec(memory_space=pl.ANY), *vmem_specs(3)),
        scratch_shapes=scratch(len(others))
        + [
            pltpu.VMEM((96, count), f32),
            pick_for(sent),
            pltpu.VMEM((3, count), f32),
            pltpu.SemaphoreType.DMA,
        ],
        compiler_params=params,
        cost_estimate=cost(len(others)),
        name="other_pairs_and_deposit",
    )(
        positions,
        sources,
        own_sums,
        dye_amount[None],
        cell_fraction,
        cell_index[None],
        tile_row,
        owner_row,
        *others,
    )
    deposit = lambda slots, name: pl.pallas_call(
        functools.partial(deposit_kernel, tiles, owners, slots),
        out_shape=rows_for(slots),
        in_specs=vmem_specs(4),
        out_specs=vmem_specs(1)[0],
        scratch_shapes=[pick_for(slots)],
        compiler_params=params,
        cost_estimate=pl.CostEstimate(
            flops=len(slots) * tiles * 8 * count * 256 * 2,
            bytes_accessed=count * 1024,
            transcendentals=0,
        ),
        name=name,
    )(value, spread, tile_row, owner_row).reshape(len(slots), tiles, 4, 128)
    exchange = lambda x, s: lax.ppermute(x, "dom", [(i, i ^ s) for i in range(owners)])
    arrived = exchange(send.reshape(len(sent), tiles, 4, 128), 1)
    grid = deposit(kept, "deposit_kept_slots") + arrived
    if owners == 8:
        far = exchange(grid[0], 6)
        near = lax.ppermute(grid[1:], "dom", [(i, i ^ (4 if i & 1 else 2)) for i in range(owners)])
        own = deposit(apart, "deposit_chip_slots")
        over = exchange(own[1] + near[1], 1)
        return velocity, own[0] + near[0] + far + over
    got = [exchange(grid[j], 2 * j) for j in range(owners // 2 - 1, 0, -1)]
    return velocity, sum(got, grid[0])


def solution(mesh):
    both = ("dom", "blk")
    placed = (
        P(None, both),
        P(None, both),
        P(both),
        P(both),
        P(None, both),
        P(both),
        P(both),
        P(both, None),
    )
    return jax.shard_map(
        on_device,
        mesh=mesh,
        in_specs=placed,
        out_specs=(P(None, both), P(both, None, None)),
        check_vma=False,
    )
```

```python
import functools
import math

import jax
import jax.numpy as jnp
from jax import lax
from jax.experimental import pallas as pl
from jax.experimental.pallas import tpu as pltpu
from jax.sharding import PartitionSpec as P

time_step = 0.02
move_scale = 2.0
inverse_volume = 32.0
kernel_scale = 1.0 / (4.0 * math.pi)
f32 = jnp.float32
bf16 = jnp.bfloat16
transposed_rhs = (((1,), (1,)), ((), ()))


def split3(x):
    high = x.astype(bf16)
    rest = x - high.astype(f32)
    middle = rest.astype(bf16)
    return high, middle, (rest - middle.astype(f32)).astype(bf16)


def rows_of(array, first, count):
    return [array[first + d : first + d + 1] for d in range(count)]


def cross_rows(left, right):
    return [
        left[1] * right[2] - left[2] * right[1],
        left[2] * right[0] - left[0] * right[2],
        left[0] * right[1] - left[1] * right[0],
    ]


def square_sum(rows):
    return rows[0] * rows[0] + rows[1] * rows[1] + rows[2] * rows[2]


def target_features(points):
    one = jnp.ones_like(points[0])
    zero = jnp.zeros_like(one)
    stack = jnp.concatenate(points + [one, square_sum(points), zero, zero, zero], axis=0)
    high, middle, low = [part.astype(f32) for part in split3(stack)]
    return jnp.concatenate([high, middle, high, low, high, middle], axis=0).astype(bf16)


def centered(pos, center):
    return rows_of(pos - center, 0, 3)


def center_of(pos):
    return jnp.mean(pos, axis=1, keepdims=True)


def source_features(src, center):
    points = centered(src[0:3], center)
    vortex = rows_of(src, 3, 3)
    radius = src[6:7]
    offset = square_sum(points) + radius * radius
    one = jnp.ones_like(radius)
    zero = jnp.zeros_like(radius)
    stack = jnp.concatenate([-2.0 * p for p in points] + [offset, one, zero, zero, zero], axis=0)
    high, middle, low = [part.astype(f32) for part in split3(stack)]
    features = jnp.concatenate([high, high, middle, high, low, middle], axis=0)
    base = jnp.concatenate(vortex + cross_rows(vortex, points), axis=0)
    groups = jnp.concatenate(
        [base] + [base * p for p in points] + [base * offset, zero, zero], axis=0
    )
    return features.T.astype(bf16), jnp.concatenate(split3(groups), axis=0)


def add_pair_sums(lag, unroll, target_ref, feature_ref, moment_ref, sum_ref, slope_ref):
    targets = sum_ref.shape[1]
    slots, chunk, width = slope_ref.shape
    chunk = chunk // 2
    chunks = feature_ref.shape[0] // chunk
    tiles = targets // width
    lag = min(lag, chunks)

    def produce(start, number):
        square = jnp.dot(
            feature_ref[number * chunk : (number + 1) * chunk, :],
            target_ref[:, pl.ds(start, width)],
            preferred_element_type=f32,
        )
        inverse = lax.rsqrt(square)
        inverse2 = inverse * inverse
        slope = inverse2 * inverse2 * inverse
        high = slope.astype(bf16)
        slope_ref[number % slots, :chunk] = high
        slope_ref[number % slots, chunk:] = (slope - high.astype(f32)).astype(bf16)

    def consume(start, number):
        moments = moment_ref[:, number * chunk : (number + 1) * chunk]
        sum_ref[:, pl.ds(start, width)] += jnp.dot(
            moments, slope_ref[number % slots, :chunk], preferred_element_type=f32
        ) + jnp.dot(moments, slope_ref[number % slots, chunk:], preferred_element_type=f32)

    if tiles > unroll:
        for number in range(chunks - lag, chunks):
            slope_ref[number % slots] = jnp.zeros(slope_ref.shape[1:], bf16)

    def step(k, carry):
        for u in range(unroll):
            start = pl.multiple_of((k * unroll + u) * width, width)
            before = pl.multiple_of(jnp.maximum(k * unroll + u - 1, 0) * width, width)
            for number in range(chunks):
                if number >= lag:
                    consume(start, number - lag)
                elif u > 0 or tiles > unroll:
                    consume(before, number - lag + chunks)
                produce(start, number)
        return carry

    if tiles > unroll:
        lax.fori_loop(0, tiles // unroll, step, 0)
    else:
        step(0, 0)
    for number in range(chunks - lag, chunks):
        consume((tiles - 1) * width, number)


def own_kernel(
    pos_ref, src_ref, sum_ref, target_ref, feature_ref, moment_ref, slope_ref
):
    center = center_of(pos_ref[...])
    target_ref[...] = target_features(centered(pos_ref[...], center))
    feature_ref[...], moment_ref[...] = source_features(src_ref[...], center)
    sum_ref[...] = jnp.zeros_like(sum_ref)
    tiles = sum_ref.shape[1] // slope_ref.shape[2]
    add_pair_sums(
        8, math.gcd(tiles, 8), target_ref, feature_ref, moment_ref, sum_ref, slope_ref
    )


def combine(points, vortex, sums):
    plain, by_x, by_y, by_z, by_offset = [sums[6 * k : 6 * k + 6] for k in range(5)]
    kernel = (
        square_sum(points) * plain
        + by_offset
        - 2.0 * (points[0] * by_x + points[1] * by_y + points[2] * by_z)
    ) * kernel_scale
    along = points[0] * vortex[0] + points[1] * vortex[1] + points[2] * vortex[2]
    slope = (along * plain - vortex[0] * by_x - vortex[1] * by_y - vortex[2] * by_z) * (
        -3.0 * kernel_scale
    )
    kernel_a = rows_of(kernel, 0, 3)
    velocity = [u - v for u, v in zip(cross_rows(kernel_a, points), rows_of(kernel, 3, 3))]
    term_one = cross_rows(kernel_a, vortex)
    slope_a = rows_of(slope, 0, 3)
    term_two = [u - v for u, v in zip(cross_rows(slope_a, points), rows_of(slope, 3, 3))]
    return velocity, [u + v for u, v in zip(term_one, term_two)]


def axis_weights(node, base, fraction, cells):
    t = fraction
    s = 1.0 - t
    inner = [1.0 - 2.5 * u * u + 1.5 * u * u * u for u in (t, s)]
    weights = [-0.5 * s * s * t, inner[0], inner[1], -0.5 * t * t * s]
    place = (node - base + 1) & (cells - 1)
    out = jnp.zeros(node.shape, f32)
    for k in range(4):
        out = jnp.where(place == k, weights[k], out)
    return out


def tail_kernel(
    tiles,
    owners,
    pos_ref,
    src_ref,
    before_ref,
    dye_ref,
    frac_ref,
    cell_ref,
    tile_ref,
    owner_ref,
    *refs,
):
    other_refs = refs[:-12]
    velocity_ref, value_ref, spread_ref, send_ref, *refs = refs[-12:]
    target_ref, feature_ref, moment_ref, slope_ref, sum_ref, pick_ref, ready_ref, copied = refs
    count = src_ref.shape[1]
    center = center_of(pos_ref[...])
    points = centered(pos_ref[...], center)
    target_ref[...] = target_features(points)
    for k, other_ref in enumerate(other_refs):
        place = slice(k * count, (k + 1) * count)
        feature_ref[place], moment_ref[:, place] = source_features(other_ref[...], center)
    sum_ref[...] = before_ref[...]
    add_pair_sums(
        8,
        math.gcd(count // slope_ref.shape[2], 2),
        target_ref,
        feature_ref,
        moment_ref,
        sum_ref,
        slope_ref,
    )
    sums = sum_ref[0:32, :] + sum_ref[32:64, :] + sum_ref[64:96, :]
    vortex = rows_of(src_ref[...], 3, 3)
    velocity, stretch = combine(points, vortex, sums)
    ready_ref[...] = jnp.concatenate(velocity, axis=0)
    velocity_copy = pltpu.make_async_copy(ready_ref, velocity_ref, copied)
    velocity_copy.start()

    values = [inverse_volume * (a + time_step * d) for a, d in zip(vortex, stretch)]
    values.append(inverse_volume * dye_ref[...])
    cell = cell_ref[...]
    starts = [cell & 7, (cell >> 3) & 3, cell >> 5]
    bases, fractions = [], []
    for d in range(3):
        place = starts[d].astype(f32) + frac_ref[d : d + 1, :] + move_scale * velocity[d]
        lowest = jnp.floor(place)
        bases.append(lowest.astype(jnp.int32))
        fractions.append(place - lowest)
    node = lax.broadcasted_iota(jnp.int32, (8, count), 0)
    weight_x = axis_weights(node, bases[0], fractions[0], 8)
    node = lax.broadcasted_iota(jnp.int32, (16, count), 0)
    weight_zy = axis_weights(node & 3, bases[1], fractions[1], 4) * axis_weights(
        node >> 2, bases[2], fractions[2], 4
    )
    spread = jnp.concatenate([weight_zy[k : k + 1] * weight_x for k in range(16)], axis=0)
    spread_high = spread.astype(bf16)
    spread_low = (spread - spread_high.astype(f32)).astype(bf16)
    spread_both = jnp.concatenate([spread_high, spread_low], axis=0)

    value_ref[...] = jnp.concatenate(values, axis=0)
    spread_ref[...] = spread_both
    send_ref[...] = deposits(
        tiles,
        owners,
        slots_of(owners)[0],
        owner_ref[...],
        tile_ref[...],
        value_ref[...],
        spread_both,
        pick_ref,
    )
    velocity_copy.wait()


def slots_of(owners):
    if owners == 8:
        return (7, 5, 4), (6, 2, 3), (0, 1)
    return tuple(range(1, owners, 2)), tuple(range(0, owners, 2)), ()


def deposits(tiles, owners, slots, owner, tile, value, spread_both, pick_ref):
    count = owner.shape[1]
    me = lax.axis_index("dom")
    slot = owner ^ me
    if owners == 8:
        traded = (slot & 1) | ((slot & 2) << 1) | ((slot & 4) >> 1)
        slot = jnp.where((me & 1) == 1, traded, slot)
    number = jnp.full(slot.shape, -8, jnp.int32)
    for place, s in enumerate(slots):
        number = jnp.where(slot == s, place * tiles + tile, number)
    node = lax.broadcasted_iota(jnp.int32, (16, count), 0)
    mine = number - (node >> 2)
    value = jnp.concatenate([value] * 4, axis=0)
    value_high = value.astype(bf16).astype(f32)
    value_low = value - value_high
    total = len(slots) * tiles * 4
    for group in range(total // 16):
        mask = mine == 4 * group
        first = 16 * group
        pick_ref[first : first + 16, :] = jnp.where(mask, value_high, 0.0).astype(bf16)
        first = total + 16 * group
        pick_ref[first : first + 16, :] = jnp.where(mask, value_low, 0.0).astype(bf16)
    both = lax.dot_general(
        pick_ref[...], spread_both, transposed_rhs, preferred_element_type=f32
    )
    both = both[:, 0:128] + both[:, 128:256]
    return both[:total] + both[total:]


def deposit_kernel(
    tiles, owners, slots, value_ref, spread_ref, tile_ref, owner_ref, out_ref, pick_ref
):
    out_ref[...] = deposits(
        tiles,
        owners,
        slots,
        owner_ref[...],
        tile_ref[...],
        value_ref[...],
        spread_ref[...],
        pick_ref,
    )


def vmem_specs(count):
    return [pl.BlockSpec(memory_space=pltpu.VMEM)] * count


def partner(i, step, count):
    return i ^ step if count & (count - 1) == 0 else (i + step) % count


def on_device(
    positions, strength, core_radius, dye_amount, cell_fraction, cell_index, tile_local, owner_dom
):
    count = positions.shape[1]
    tiles = count // 128
    owners = lax.axis_size("dom")
    blocks = lax.axis_size("blk")
    width = math.gcd(count, 256)
    sources = jnp.concatenate([positions, strength, core_radius[None]], axis=0)
    others = [
        lax.ppermute(sources, "blk", [(i, partner(i, s, blocks)) for i in range(blocks)])
        for s in range(1, blocks)
    ]
    scratch = lambda n: [
        pltpu.VMEM((48, count), bf16),
        pltpu.VMEM((n * count, 48), bf16),
        pltpu.VMEM((96, n * count), bf16),
        pltpu.VMEM((min(8, count // width), 2 * width, width), bf16),
    ]
    params = pltpu.CompilerParams(vmem_limit_bytes=48 * 2**20)
    cost = lambda n: pl.CostEstimate(
        flops=n * count * count * 256 * 2 * 3,
        bytes_accessed=4 * count * 256,
        transcendentals=n * count * count,
    )
    own_sums = pl.pallas_call(
        own_kernel,
        out_shape=jax.ShapeDtypeStruct((96, count), f32),
        in_specs=vmem_specs(2),
        out_specs=vmem_specs(1)[0],
        scratch_shapes=scratch(1),
        compiler_params=params,
        cost_estimate=cost(1),
        name="own_pairs",
    )(positions, sources)
    sent, kept, apart = slots_of(owners)
    rows_for = lambda slots: jax.ShapeDtypeStruct((len(slots) * tiles * 4, 128), f32)
    pick_for = lambda slots: pltpu.VMEM((len(slots) * tiles * 8, count), bf16)
    tile_row = tile_local[None]
    owner_row = owner_dom.reshape(1, count)
    velocity, value, spread, send = pl.pallas_call(
        functools.partial(tail_kernel, tiles, owners),
        out_shape=(
            jax.ShapeDtypeStruct((3, count), f32),
            jax.ShapeDtypeStruct((4, count), f32),
            jax.ShapeDtypeStruct((256, count), bf16),
            rows_for(sent),
        ),
        in_specs=vmem_specs(8 + len(others)),
        out_specs=(pl.BlockSpec(memory_space=pl.ANY), *vmem_specs(3)),
        scratch_shapes=scratch(len(others))
        + [
            pltpu.VMEM((96, count), f32),
            pick_for(sent),
            pltpu.VMEM((3, count), f32),
            pltpu.SemaphoreType.DMA,
        ],
        compiler_params=params,
        cost_estimate=cost(len(others)),
        name="other_pairs_and_deposit",
    )(
        positions,
        sources,
        own_sums,
        dye_amount[None],
        cell_fraction,
        cell_index[None],
        tile_row,
        owner_row,
        *others,
    )
    deposit = lambda slots, name: pl.pallas_call(
        functools.partial(deposit_kernel, tiles, owners, slots),
        out_shape=rows_for(slots),
        in_specs=vmem_specs(4),
        out_specs=vmem_specs(1)[0],
        scratch_shapes=[pick_for(slots)],
        compiler_params=params,
        cost_estimate=pl.CostEstimate(
            flops=len(slots) * tiles * 8 * count * 256 * 2,
            bytes_accessed=count * 1024,
            transcendentals=0,
        ),
        name=name,
    )(value, spread, tile_row, owner_row).reshape(len(slots), tiles, 4, 128)
    exchange = lambda x, s: lax.ppermute(x, "dom", [(i, i ^ s) for i in range(owners)])
    arrived = exchange(send.reshape(len(sent), tiles, 4, 128), 1)
    grid = deposit(kept, "deposit_kept_slots") + arrived
    if owners == 8:
        far = exchange(grid[0], 6)
        near = lax.ppermute(grid[1:], "dom", [(i, i ^ (4 if i & 1 else 2)) for i in range(owners)])
        own = deposit(apart, "deposit_chip_slots")
        over = exchange(own[1] + near[1], 1)
        return velocity, own[0] + near[0] + far + over
    got = [exchange(grid[j], 2 * j) for j in range(owners // 2 - 1, 0, -1)]
    return velocity, sum(got, grid[0])


def solution(mesh):
    both = ("dom", "blk")
    placed = (
        P(None, both),
        P(None, both),
        P(both),
        P(both),
        P(None, both),
        P(both),
        P(both),
        P(both, None),
    )
    return jax.shard_map(
        on_device,
        mesh=mesh,
        in_specs=placed,
        out_specs=(P(None, both), P(both, None, None)),
        check_vma=False,
    )
```
